256 devices in a mesh: wide: 16 (over x, y_lo, core), narrow: 16 (over z, y_hi).
Axes of the slice: x: 4, y: 4 (y_hi: 2, y_lo: 2; y = y_hi * 2 + y_lo), z: 8, core: 2. Of those that a mesh axis runs over, the one named last changes fastest.
Arguments:
- hamiltonian_tiles: float32 [24576, 24576], P('wide', 'narrow'), may hold values from -0.02734375 to 0.02734375
- row_columns: int32 [16, 16], P('wide'), may hold values from 0 to 15, as said below
- start_vectors: float32 [24576, 128], P(('wide', 'narrow')), may hold values from -60 to 60
Outputs:
- new_vectors: float32 [24576, 128], P(('wide', 'narrow'))
The draws below stay inside these ranges and needn't reach their ends.
Inputs may be any that keep to these rules, and one draw needn't show every extreme that they name: For block row r = w + j // 16, row_columns[w, j] = (r + d) mod 16, with d = 0 where j % 16 = 0 and, for the other tiles of that block row, distinct d between 1 and 15; a block's mirror may also be stored.
All inputs are finite; a program needn't handle non-finite values.
Results may differ from the reference program's by a relative error of at most 0.0003.
Values sent between devices are 32-bit elements; how exact they have to be, the bound alone decides.
No kernel may reach another device: no remote copies, remote signals or barrier semaphores. Data moves between devices by JAX's collectives and lax.ppermute only.
A program may use at most 64 MiB of HBM per device.

```python
import jax
import jax.numpy as jnp
from jax import lax

B = 1536
K = 128
ITERS = 2
NS_STEPS = 5
TILES_ROW = 16
NB = 16
N_WIDE = 16
N_NARROW = 16


def draw_row_columns(key, part):
    rows_group = N_NARROW // TILES_ROW
    blocks = N_WIDE * rows_group
    half = blocks // 2
    count = blocks - 2
    candidates = jnp.arange(count, dtype=jnp.int32) + 1
    scores = jax.random.randint(jax.random.fold_in(key, 11), (blocks, count), 0, 1048576)
    scores = scores * blocks + jnp.arange(count, dtype=jnp.int32)[None, :]
    scores = jnp.where(candidates[None, :] == half, 2000000000, scores)
    order = jnp.argsort(scores, axis=1).astype(jnp.int32)
    randoms = order[:, :TILES_ROW - 3] + 1
    fixed = jnp.concatenate([jnp.zeros((blocks, 1), jnp.int32), jnp.full((blocks, 1), half, jnp.int32), jnp.full((blocks, 1), blocks - 1, jnp.int32)], axis=1)
    offsets = jnp.concatenate([fixed, randoms], axis=1)
    rows = jnp.arange(blocks, dtype=jnp.int32)[:, None]
    return ((rows + offsets) % blocks).reshape(N_WIDE, N_NARROW).astype(jnp.int32)


def draw_start_vectors(key, part):
    column_key = jax.random.fold_in(key, 21)
    entry_key = jax.random.fold_in(key, 22)
    column_scale = 10.0 ** jax.random.uniform(column_key, (1, K), jnp.float32, 0.0, 1.0)
    entries = jax.random.normal(entry_key, (NB * B, K), jnp.float32)
    values = entries * column_scale
    return jnp.clip(values, -60.0, 60.0).astype(jnp.float32)


def level_of(own_key, shape, cuts, least, largest):
    def one(position, blocks):
        draws = jax.random.uniform(jax.random.fold_in(jax.random.fold_in(own_key, 6), position), (blocks,), jnp.float32, least / len(cuts), largest / len(cuts))
        return jnp.repeat(jnp.exp(draws), shape[position] // blocks).reshape((-1,) + (1,) * (len(shape) - position - 1))

    loudness = one(*cuts[0])
    for cut in cuts[1:]:
        loudness = loudness * one(*cut)
    return loudness


def bell_draw(rng, dims, deviation, bound, cuts=(), kind=jnp.bfloat16):
    drawn = jax.random.normal(rng, dims, jnp.float32) * deviation
    if len(cuts) > 0:
        drawn = level_of(rng, dims, cuts, -0.22, 0.18) * drawn
    return jnp.clip(drawn, min=-bound, max=bound).astype(kind)


def setup_inputs(seed: int = 0) -> dict:
    seeds = jax.random.split(jax.random.key(seed), 4)
    return {
        "hamiltonian_tiles": bell_draw(seeds[0], (N_WIDE * B, N_NARROW * B), (2 * B * TILES_ROW) ** -0.5, 0.02734375, ((0, 16), (1, 16)), jnp.float32),
        "row_columns": draw_row_columns(jax.random.fold_in(seeds[3], 71), 0),
        "start_vectors": draw_start_vectors(jax.random.fold_in(seeds[3], 71), 0),
    }


def apply_hamiltonian(tiles, columns, vectors):
    rows_group = N_NARROW // TILES_ROW
    blocks = vectors.reshape(NB, B, K)
    grouped = tiles.reshape(N_WIDE, B, N_NARROW, B)
    owned = blocks.reshape(N_WIDE, rows_group, B, K)

    def one_group(carry, inputs):
        group_tiles, group_cols, own_blocks = inputs
        quad = group_tiles.reshape(B, rows_group, TILES_ROW, B)
        cols = group_cols.astype(jnp.int32).reshape(rows_group, TILES_ROW)
        column_blocks = blocks[cols]
        direct = jnp.einsum('iqtj,qtjk->qik', quad, column_blocks, precision=lax.Precision.HIGHEST)
        transposed = jnp.einsum('iqtj,qik->qtjk', quad, own_blocks, precision=lax.Precision.HIGHEST)
        carry = carry.at[cols.reshape(N_NARROW)].add(transposed.reshape(N_NARROW, B, K))
        return (carry, direct)
    zeros = jnp.zeros((NB, B, K), jnp.float32)
    moved, direct_rows = lax.scan(one_group, zeros, (grouped, columns, owned))
    return (direct_rows.reshape(NB, B, K) + moved).reshape(NB * B, K)

def orthonormalize(product, gram):
    identity = jnp.eye(K, dtype=jnp.float32)
    scale = jnp.sqrt(jnp.sum(gram * gram) + 1e-06)
    current = gram / scale
    inverse = identity
    for repeat in range(NS_STEPS):
        middle = 1.5 * identity - 0.5 * jnp.dot(inverse, current, precision=lax.Precision.HIGHEST)
        current = jnp.dot(current, middle, precision=lax.Precision.HIGHEST)
        inverse = jnp.dot(middle, inverse, precision=lax.Precision.HIGHEST)
    return jnp.dot(product, inverse, precision=lax.Precision.HIGHEST) * jnp.sqrt(NB * B / scale)

def reference(hamiltonian_tiles, row_columns, start_vectors):
    vectors = start_vectors
    for repeat in range(ITERS):
        product = apply_hamiltonian(hamiltonian_tiles, row_columns, vectors)
        gram = jnp.dot(product.T, product, precision=lax.Precision.HIGHEST)
        vectors = orthonormalize(product, gram)
    return vectors
```

```python
import jax
import jax.numpy as jnp
from jax import lax
from jax.experimental import pallas as pl
from jax.experimental.pallas import tpu as pltpu
from jax.sharding import PartitionSpec as P

NS_STEPS = 5
WIDE, NARROW = "wide", "narrow"
HIGH = lax.Precision.HIGH
HIGHEST = lax.Precision.HIGHEST


def exchange(parts, axis):
    return lax.all_to_all(parts, axis, 0, 0, tiled=True)


def to_everyone(value, axis):
    return exchange(jnp.broadcast_to(value[None], (lax.axis_size(axis), *value.shape)), axis)


def move_blocks(blocks, columns, scatter):
    count = blocks.shape[0]

    def kernel(columns_ref, blocks_ref, moved_ref):
        for i in range(count):
            column = columns_ref[i]
            if scatter:
                moved_ref[column] = blocks_ref[i]
            else:
                moved_ref[i] = blocks_ref[column]

    return pl.pallas_call(
        kernel,
        out_shape=jax.ShapeDtypeStruct(blocks.shape, blocks.dtype),
        in_specs=[
            pl.BlockSpec(memory_space=pltpu.SMEM),
            pl.BlockSpec(memory_space=pltpu.VMEM),
        ],
        out_specs=pl.BlockSpec(memory_space=pltpu.VMEM),
        cost_estimate=pl.CostEstimate(flops=0, bytes_accessed=8 * blocks.size, transcendentals=0),
    )(columns, blocks)


def apply_hamiltonian(tile, columns, vectors):
    rows, width = vectors.shape
    count = lax.axis_size(NARROW)
    with jax.named_scope("gather_wide"):
        slices = to_everyone(vectors, WIDE)
    with jax.named_scope("gather_row"):
        row_block = to_everyone(vectors, NARROW).reshape(count * rows, width)
    with jax.named_scope("gather_column"):
        picked = move_blocks(slices, columns, scatter=False)
        column_block = exchange(picked, NARROW).reshape(count * rows, width)
    with jax.named_scope("transposed"):
        transposed = lax.dot_general(tile, row_block, (((0,), (0,)), ((), ())), precision=HIGH)
    with jax.named_scope("direct"):
        direct = jnp.dot(tile, column_block, precision=HIGH)
    with jax.named_scope("back_transposed"):
        arrived = exchange(transposed.reshape(count, rows, width), NARROW)
        placed = move_blocks(arrived, columns, scatter=True)
    with jax.named_scope("back_direct"):
        direct_sum = exchange(direct.reshape(count, rows, width), NARROW).sum(axis=0)
    with jax.named_scope("back_wide"):
        transposed_sum = exchange(placed, WIDE).sum(axis=0)
    return direct_sum + transposed_sum


def sum_of_everyone(value):
    for axis in (WIDE, NARROW):
        size = lax.axis_size(axis)
        step = 1
        while step < size:
            value = value + lax.ppermute(value, axis, [(i, i ^ step) for i in range(size)])
            step *= 2
    return value


def inverse_root(gram, total_rows):
    identity = jnp.eye(gram.shape[0], dtype=jnp.float32)
    scale = jnp.sqrt(jnp.sum(gram * gram) + 1e-06)
    current = gram / scale
    inverse = identity
    for repeat in range(NS_STEPS):
        middle = 1.5 * identity - 0.5 * jnp.dot(inverse, current, precision=HIGHEST)
        current = jnp.dot(current, middle, precision=HIGHEST)
        inverse = jnp.dot(middle, inverse, precision=HIGHEST)
    return inverse * jnp.sqrt(total_rows / scale)


def gram_of(value):
    return lax.dot_general(value, value, (((0,), (0,)), ((), ())), precision=HIGHEST)


def on_device(tile, row_columns, start_vectors):
    total_rows = float(lax.axis_size(WIDE) * lax.axis_size(NARROW) * start_vectors.shape[0])
    columns = row_columns[0]
    first = apply_hamiltonian(tile, columns, start_vectors)
    second = apply_hamiltonian(tile, columns, first)
    with jax.named_scope("grams"):
        grams = sum_of_everyone(jnp.concatenate([gram_of(first), gram_of(second)], axis=0))
        gram_first, gram_second = jnp.split(grams, 2, axis=0)
    with jax.named_scope("inverse_first"):
        root_first = inverse_root(gram_first, total_rows)
    with jax.named_scope("inverse_second"):
        gram = jnp.dot(
            root_first.T, jnp.dot(gram_second, root_first, precision=HIGHEST), precision=HIGHEST
        )
        root_second = inverse_root(gram, total_rows)
    with jax.named_scope("finish"):
        return jnp.dot(
            jnp.dot(second, root_first, precision=HIGHEST), root_second, precision=HIGHEST
        )


def solution(mesh):
    return jax.shard_map(
        on_device,
        mesh=mesh,
        in_specs=(P(WIDE, NARROW), P(WIDE, None), P((WIDE, NARROW), None)),
        out_specs=P((WIDE, NARROW), None),
        check_vma=False,
    )
```

```python
import jax
import jax.numpy as jnp
from jax import lax
from jax.experimental import pallas as pl
from jax.experimental.pallas import tpu as pltpu
from jax.sharding import PartitionSpec as P

NS_STEPS = 5
WIDE, NARROW = "wide", "narrow"
HIGH = lax.Precision.HIGH
HIGHEST = lax.Precision.HIGHEST


def exchange(parts, axis):
    return lax.all_to_all(parts, axis, 0, 0, tiled=True)


def to_everyone(value, axis):
    return exchange(jnp.broadcast_to(value[None], (lax.axis_size(axis), *value.shape)), axis)


def move_blocks(blocks, columns, scatter):
    count = blocks.shape[0]

    def kernel(columns_ref, blocks_ref, moved_ref):
        for i in range(count):
            column = columns_ref[i]
            if scatter:
                moved_ref[column] = blocks_ref[i]
            else:
                moved_ref[i] = blocks_ref[column]

    return pl.pallas_call(
        kernel,
        out_shape=jax.ShapeDtypeStruct(blocks.shape, blocks.dtype),
        in_specs=[
            pl.BlockSpec(memory_space=pltpu.SMEM),
            pl.BlockSpec(memory_space=pltpu.VMEM),
        ],
        out_specs=pl.BlockSpec(memory_space=pltpu.VMEM),
        cost_estimate=pl.CostEstimate(flops=0, bytes_accessed=8 * blocks.size, transcendentals=0),
    )(columns, blocks)


def swap(value, axis, bit):
    size = lax.axis_size(axis)
    return lax.ppermute(value, axis, [(i, i ^ bit) for i in range(size)])


def bits_of(size):
    bit = size // 2
    while bit:
        yield bit
        bit //= 2


def relative_order(axis):
    size = lax.axis_size(axis)
    places = [0]
    for bit in bits_of(size):
        places = places + [place ^ bit for place in places]
    return lax.axis_index(axis).astype(jnp.int32) ^ jnp.array(places, jnp.int32)


def doubled(value, axis):
    held = value[None]
    for bit in bits_of(lax.axis_size(axis)):
        held = jnp.concatenate([held, swap(held, axis, bit)], axis=0)
    return held


def halved(parts, axis):
    for bit in reversed(list(bits_of(lax.axis_size(axis)))):
        half = parts.shape[0] // 2
        parts = parts[:half] + swap(parts[half:], axis, bit)
    return parts[0]


def summed(value, axis):
    for bit in bits_of(lax.axis_size(axis)):
        value = value + swap(value, axis, bit)
    return value


def apply_hamiltonian(tile, columns, order, vectors):
    rows, width = vectors.shape
    count = lax.axis_size(NARROW)
    with jax.named_scope("gather_wide"):
        slices = to_everyone(vectors, WIDE)
    with jax.named_scope("gather_row"):
        row_block = move_blocks(doubled(vectors, NARROW), order, scatter=True)
        row_block = row_block.reshape(count * rows, width)
    with jax.named_scope("gather_column"):
        picked = move_blocks(slices, columns, scatter=False)
        column_block = exchange(picked, NARROW).reshape(count * rows, width)
    with jax.named_scope("transposed"):
        transposed = lax.dot_general(tile, row_block, (((0,), (0,)), ((), ())), precision=HIGH)
    with jax.named_scope("direct"):
        direct = jnp.dot(tile, column_block, precision=HIGH)
    with jax.named_scope("back_transposed"):
        arrived = exchange(transposed.reshape(count, rows, width), NARROW)
        placed = move_blocks(arrived, columns, scatter=True)
    with jax.named_scope("back_direct"):
        parts = move_blocks(direct.reshape(count, rows, width), order, scatter=False)
        direct_sum = halved(parts, NARROW)
    with jax.named_scope("back_wide"):
        transposed_sum = exchange(placed, WIDE).sum(axis=0)
    return direct_sum + transposed_sum, row_block


def inverse_root(gram, total_rows):
    identity = jnp.eye(gram.shape[0], dtype=jnp.float32)
    scale = jnp.sqrt(jnp.sum(gram * gram) + 1e-06)
    current = gram / scale
    inverse = identity
    for repeat in range(NS_STEPS):
        middle = 1.5 * identity - 0.5 * jnp.dot(inverse, current, precision=HIGHEST)
        current = jnp.dot(current, middle, precision=HIGHEST)
        inverse = jnp.dot(middle, inverse, precision=HIGHEST)
    return inverse * jnp.sqrt(total_rows / scale)


def gram_of(value):
    return lax.dot_general(value, value, (((0,), (0,)), ((), ())), precision=HIGHEST)


def on_device(tile, row_columns, start_vectors):
    total_rows = float(lax.axis_size(WIDE) * lax.axis_size(NARROW) * start_vectors.shape[0])
    columns = row_columns[0]
    order = relative_order(NARROW)
    first, _ = apply_hamiltonian(tile, columns, order, start_vectors)
    second, first_block = apply_hamiltonian(tile, columns, order, first)
    with jax.named_scope("gram_first"):
        gram_first = summed(gram_of(first_block), WIDE)
    with jax.named_scope("gram_second"):
        gram_second = summed(summed(gram_of(second), WIDE), NARROW)
    with jax.named_scope("inverse_first"):
        root_first = inverse_root(gram_first, total_rows)
    with jax.named_scope("inverse_second"):
        gram = jnp.dot(
            root_first.T, jnp.dot(gram_second, root_first, precision=HIGHEST), precision=HIGHEST
        )
        root_second = inverse_root(gram, total_rows)
    with jax.named_scope("finish"):
        return jnp.dot(
            jnp.dot(second, root_first, precision=HIGHEST), root_second, precision=HIGHEST
        )


def solution(mesh):
    return jax.shard_map(
        on_device,
        mesh=mesh,
        in_specs=(P(WIDE, NARROW), P(WIDE, None), P((WIDE, NARROW), None)),
        out_specs=P((WIDE, NARROW), None),
        check_vma=False,
    )
```

```python
import jax
import jax.numpy as jnp
from jax import lax
from jax.experimental import pallas as pl
from jax.experimental.pallas import tpu as pltpu
from jax.sharding import PartitionSpec as P

NS_STEPS = 5
WIDE, NARROW = "wide", "narrow"
HIGHEST = lax.Precision.HIGHEST


def exchange(parts, axis):
    return lax.all_to_all(parts, axis, 0, 0, tiled=True)


def to_everyone(value, axis):
    return exchange(jnp.broadcast_to(value[None], (lax.axis_size(axis), *value.shape)), axis)


def move_blocks(blocks, columns, scatter):
    count = blocks.shape[0]

    def kernel(columns_ref, blocks_ref, moved_ref, done):
        copies = []
        for i in range(count):
            column = columns_ref[i]
            source, target = (i, column) if scatter else (column, i)
            copies.append(
                pltpu.make_async_copy(blocks_ref.at[source], moved_ref.at[target], done.at[i])
            )
        for copy in copies:
            copy.start()
        for copy in copies:
            copy.wait()

    return pl.pallas_call(
        kernel,
        out_shape=jax.ShapeDtypeStruct(blocks.shape, blocks.dtype),
        in_specs=[pl.BlockSpec(memory_space=pltpu.SMEM), pl.BlockSpec(memory_space=pl.ANY)],
        out_specs=pl.BlockSpec(memory_space=pl.ANY),
        scratch_shapes=[pltpu.SemaphoreType.DMA((count,))],
        compiler_params=pltpu.CompilerParams(vmem_limit_bytes=1 << 20),
        cost_estimate=pl.CostEstimate(flops=0, bytes_accessed=8 * blocks.size, transcendentals=0),
    )(columns, blocks)


def high_low(value):
    high = value.astype(jnp.bfloat16)
    return high, (value - high.astype(jnp.float32)).astype(jnp.bfloat16)


def product_of(left, right):
    return jnp.dot(left, right, preferred_element_type=jnp.float32)


def kernel_cost(tile, width):
    return pl.CostEstimate(flops=3 * tile.size * width, bytes_accessed=2 * tile.size, transcendentals=0)


def direct_half(tile, column_block, half, places):
    groups, _, rows, order = tile.shape
    width = column_block.shape[1]
    steps = 2
    each = groups // steps

    def kernel(where_ref, tile_ref, column_ref, out_ref, both):
        step = pl.program_id(0)

        @pl.when(step == 0)
        def _():
            high, low = high_low(column_ref[...])
            both[:, :width] = high
            both[:, width:] = low

        high, low = high_low(tile_ref[...].reshape(each * rows, order))
        wide = product_of(high, both[...])
        total = wide[:, :width] + wide[:, width:] + product_of(low, both[:, :width])
        for k in range(each):
            out_ref[where_ref[1 + step * each + k]] = total[k * rows : (k + 1) * rows]

    return pl.pallas_call(
        kernel,
        out_shape=jax.ShapeDtypeStruct((groups, rows, width), jnp.float32),
        grid_spec=pltpu.PrefetchScalarGridSpec(
            num_scalar_prefetch=1,
            grid=(steps,),
            in_specs=[
                pl.BlockSpec((each, 1, rows, order), lambda g, where: (g, where[0], 0, 0)),
                pl.BlockSpec((order, width), lambda g, where: (0, 0)),
            ],
            out_specs=pl.BlockSpec((groups, rows, width), lambda g, where: (0, 0, 0)),
            scratch_shapes=[pltpu.VMEM((order, 2 * width), jnp.bfloat16)],
        ),
        compiler_params=pltpu.CompilerParams(vmem_limit_bytes=60 << 20),
        cost_estimate=kernel_cost(tile, width),
    )(jnp.concatenate([half[None], places]), tile, column_block)


def transposed_half(tile, row_half, half, places, partial=None):
    groups, _, rows, order = tile.shape
    width = row_half.shape[2]
    depth = groups * rows
    steps = 3
    chunk = order // steps

    def kernel(where_ref, tile_ref, row_ref, *rest):
        partial_ref, (out_ref, gathered, both) = (rest[0], rest[1:]) if partial is not None else (None, rest)

        @pl.when(pl.program_id(0) == 0)
        def _():
            for k in range(groups):
                gathered[k * rows : (k + 1) * rows] = row_ref[where_ref[1 + k]]
            high, low = high_low(gathered[...].T)
            both[:width] = high
            both[width:] = low

        high, low = high_low(tile_ref[...].reshape(depth, chunk))
        wide = product_of(both[...], high)
        total = wide[:width] + wide[width:] + product_of(both[:width], low)
        if partial_ref is None:
            out_ref[...] = total
        else:
            out_ref[...] = (total + partial_ref[...]).T

    flat = pl.BlockSpec((width, chunk), lambda g, where: (0, g))
    return pl.pallas_call(
        kernel,
        out_shape=jax.ShapeDtypeStruct((width, order) if partial is None else (order, width), jnp.float32),
        grid_spec=pltpu.PrefetchScalarGridSpec(
            num_scalar_prefetch=1,
            grid=(steps,),
            in_specs=[
                pl.BlockSpec((groups, 1, rows, chunk), lambda g, where: (0, where[0], 0, g)),
                pl.BlockSpec((groups, rows, width), lambda g, where: (0, 0, 0)),
            ]
            + ([] if partial is None else [flat]),
            out_specs=flat if partial is None else pl.BlockSpec((chunk, width), lambda g, where: (g, 0)),
            scratch_shapes=[
                pltpu.VMEM((depth, width), jnp.float32),
                pltpu.VMEM((2 * width, depth), jnp.bfloat16),
            ],
        ),
        compiler_params=pltpu.CompilerParams(vmem_limit_bytes=60 << 20),
        cost_estimate=kernel_cost(tile, width),
    )(jnp.concatenate([half[None], places]), tile, row_half, *([] if partial is None else [partial]))


def swap(value, axis, bit):
    size = lax.axis_size(axis)
    return lax.ppermute(value, axis, [(i, i ^ bit) for i in range(size)])


def bits_of(size):
    bit = size // 2
    while bit:
        yield bit
        bit //= 2


def relative_places(mine, groups):
    offset = jnp.arange(groups, dtype=jnp.int32) ^ mine
    count = groups.bit_length() - 1
    return sum(((offset >> k) & 1) << (count - 1 - k) for k in range(count))


def doubled(held, axis, bits):
    for bit in bits:
        held = jnp.concatenate([held, swap(held, axis, bit)], axis=0)
    return held


def halved(mine, got, axis):
    for bit in reversed(list(bits_of(lax.axis_size(axis)))):
        if bit > 1:
            half = mine.shape[0] // 2
            sent = mine[half:] + got[half:]
            mine, got = mine[:half] + got[:half], swap(sent, axis, bit)
    return mine[0] + got[0]


def summed(value, axis):
    for bit in bits_of(lax.axis_size(axis)):
        value = value + swap(value, axis, bit)
    return value


def apply_hamiltonian(tile, columns, vectors):
    rows, width = vectors.shape
    count = lax.axis_size(NARROW)
    order = tile.shape[0]
    groups = count // 2
    me = lax.axis_index(NARROW).astype(jnp.int32)
    near, far = me & 1, (me & 1) ^ 1
    places = relative_places(me >> 1, groups)
    tile = tile.reshape(groups, 2, rows, order)
    with jax.named_scope("gather_wide"):
        slices = to_everyone(vectors, WIDE)
    bits = list(bits_of(groups))
    with jax.named_scope("gather_row"):
        near_rows = doubled(vectors[None], NARROW, [2 * bit for bit in bits[:2]])
        slices, near_rows = lax.optimization_barrier((slices, near_rows))
        near_rows = doubled(near_rows, NARROW, [2 * bit for bit in bits[2:]])
        far_rows = swap(near_rows, NARROW, 1)
    with jax.named_scope("gather_column"):
        picked = move_blocks(slices, columns, scatter=False)
        column_block = exchange(picked, NARROW).reshape(order, width)
    with jax.named_scope("transposed"):
        partial = transposed_half(tile, near_rows, near, places)
        transposed = transposed_half(tile, far_rows, far, places, partial)
    with jax.named_scope("back_transposed"):
        arrived = exchange(transposed.reshape(count, rows, width), NARROW)
        placed = move_blocks(arrived, columns, scatter=True)
    with jax.named_scope("direct"):
        sent = direct_half(tile, column_block, far, places)
        got = swap(sent, NARROW, 1)
        kept = direct_half(tile, column_block, near, places)
    with jax.named_scope("back_direct"):
        direct_sum = halved(kept, got, NARROW)
    with jax.named_scope("back_wide"):
        transposed_sum = exchange(placed, WIDE).sum(axis=0)
    return direct_sum + transposed_sum, (near_rows, far_rows)


def inverse_root(gram, total_rows):
    identity = jnp.eye(gram.shape[0], dtype=jnp.float32)
    scale = jnp.sqrt(jnp.sum(gram * gram) + 1e-06)
    current = gram / scale
    inverse = identity
    for repeat in range(NS_STEPS):
        middle = 1.5 * identity - 0.5 * jnp.dot(inverse, current, precision=HIGHEST)
        current = jnp.dot(current, middle, precision=HIGHEST)
        inverse = jnp.dot(middle, inverse, precision=HIGHEST)
    return inverse * jnp.sqrt(total_rows / scale)


def gram_of(value):
    return lax.dot_general(value, value, (((0,), (0,)), ((), ())), precision=HIGHEST)


def on_device(tile, row_columns, start_vectors):
    total_rows = float(lax.axis_size(WIDE) * lax.axis_size(NARROW) * start_vectors.shape[0])
    columns = row_columns[0]
    first, _ = apply_hamiltonian(tile, columns, start_vectors)
    second, first_halves = apply_hamiltonian(tile, columns, first)
    with jax.named_scope("gram_first"):
        grams = [gram_of(half.reshape(-1, half.shape[2])) for half in first_halves]
        gram_first = summed(grams[0] + grams[1], WIDE)
    with jax.named_scope("gram_second"):
        gram_second = summed(summed(gram_of(second), WIDE), NARROW)
    with jax.named_scope("inverse_first"):
        root_first = inverse_root(gram_first, total_rows)
    with jax.named_scope("inverse_second"):
        gram = jnp.dot(
            root_first.T, jnp.dot(gram_second, root_first, precision=HIGHEST), precision=HIGHEST
        )
        root_second = inverse_root(gram, total_rows)
    with jax.named_scope("finish"):
        return jnp.dot(
            jnp.dot(second, root_first, precision=HIGHEST), root_second, precision=HIGHEST
        )


def solution(mesh):
    return jax.shard_map(
        on_device,
        mesh=mesh,
        in_specs=(P(WIDE, NARROW), P(WIDE, None), P((WIDE, NARROW), None)),
        out_specs=P((WIDE, NARROW), None),
        check_vma=False,
    )
```

```python
import jax
import jax.numpy as jnp
from jax import lax
from jax.experimental import pallas as pl
from jax.experimental.pallas import tpu as pltpu
from jax.sharding import PartitionSpec as P

NS_STEPS = 5
WIDE, NARROW = "wide", "narrow"
HIGHEST = lax.Precision.HIGHEST


def exchange(parts, axis):
    return lax.all_to_all(parts, axis, 0, 0, tiled=True)


def to_everyone(value, axis):
    return exchange(jnp.broadcast_to(value[None], (lax.axis_size(axis), *value.shape)), axis)


def move_blocks(blocks, columns, scatter, extra=None):
    count, rows, width = blocks.shape
    arrays = [blocks] if extra is None else [blocks, extra]
    more = 0 if extra is None else extra.shape[0] // count

    def kernel(columns_ref, blocks_ref, *rest):
        moved_ref, done = rest[-2:]
        copies = []
        for i in range(count):
            column = columns_ref[i]
            source, target = (i, column) if scatter else (column, i)
            copies.append(
                pltpu.make_async_copy(
                    blocks_ref.at[source], moved_ref.at[target, pl.ds(0, rows)], done.at[i]
                )
            )
            if more:
                copies.append(
                    pltpu.make_async_copy(
                        rest[0].at[pl.ds(i * more, more)],
                        moved_ref.at[i, pl.ds(rows, more)],
                        done.at[count + i],
                    )
                )
        for copy in copies:
            copy.start()
        for copy in copies:
            copy.wait()

    return pl.pallas_call(
        kernel,
        out_shape=jax.ShapeDtypeStruct((count, rows + more, width), blocks.dtype),
        in_specs=[pl.BlockSpec(memory_space=pltpu.SMEM)]
        + [pl.BlockSpec(memory_space=pl.ANY)] * len(arrays),
        out_specs=pl.BlockSpec(memory_space=pl.ANY),
        scratch_shapes=[pltpu.SemaphoreType.DMA((len(arrays) * count,))],
        compiler_params=pltpu.CompilerParams(vmem_limit_bytes=1 << 20),
        cost_estimate=pl.CostEstimate(flops=0, bytes_accessed=8 * blocks.size, transcendentals=0),
    )(columns, *arrays)


def high_low(value):
    high = value.astype(jnp.bfloat16)
    return high, (value - high.astype(jnp.float32)).astype(jnp.bfloat16)


def product_of(left, right):
    return jnp.dot(left, right, preferred_element_type=jnp.float32)


def kernel_cost(tile, width):
    return pl.CostEstimate(flops=3 * tile.size * width, bytes_accessed=2 * tile.size, transcendentals=0)


def direct_half(tile, column_block, half, places):
    groups, _, rows, order = tile.shape
    width = column_block.shape[1]
    steps = 2
    each = groups // steps

    def kernel(where_ref, tile_ref, column_ref, out_ref, both):
        step = pl.program_id(0)

        @pl.when(step == 0)
        def _():
            high, low = high_low(column_ref[...])
            both[:, :width] = high
            both[:, width:] = low

        high, low = high_low(tile_ref[...].reshape(each * rows, order))
        wide = product_of(high, both[...])
        total = wide[:, :width] + wide[:, width:] + product_of(low, both[:, :width])
        for k in range(each):
            out_ref[where_ref[1 + step * each + k]] = total[k * rows : (k + 1) * rows]

    return pl.pallas_call(
        kernel,
        out_shape=jax.ShapeDtypeStruct((groups, rows, width), jnp.float32),
        grid_spec=pltpu.PrefetchScalarGridSpec(
            num_scalar_prefetch=1,
            grid=(steps,),
            in_specs=[
                pl.BlockSpec((each, 1, rows, order), lambda g, where: (g, where[0], 0, 0)),
                pl.BlockSpec((order, width), lambda g, where: (0, 0)),
            ],
            out_specs=pl.BlockSpec((groups, rows, width), lambda g, where: (0, 0, 0)),
            scratch_shapes=[pltpu.VMEM((order, 2 * width), jnp.bfloat16)],
        ),
        compiler_params=pltpu.CompilerParams(vmem_limit_bytes=60 << 20),
        cost_estimate=kernel_cost(tile, width),
    )(jnp.concatenate([half[None], places]), tile, column_block)


def transposed_half(tile, row_half, half, places, partial=None):
    groups, _, rows, order = tile.shape
    width = row_half.shape[2]
    depth = groups * rows
    steps = 3
    chunk = order // steps

    def kernel(where_ref, tile_ref, row_ref, *rest):
        partial_ref, (out_ref, gathered, both) = (rest[0], rest[1:]) if partial is not None else (None, rest)

        @pl.when(pl.program_id(0) == 0)
        def _():
            for k in range(groups):
                gathered[k * rows : (k + 1) * rows] = row_ref[where_ref[1 + k]]
            high, low = high_low(gathered[...].T)
            both[:width] = high
            both[width:] = low

        high, low = high_low(tile_ref[...].reshape(depth, chunk))
        wide = product_of(both[...], high)
        total = wide[:width] + wide[width:] + product_of(both[:width], low)
        if partial_ref is None:
            out_ref[...] = total
        else:
            out_ref[...] = (total + partial_ref[...]).T

    flat = pl.BlockSpec((width, chunk), lambda g, where: (0, g))
    return pl.pallas_call(
        kernel,
        out_shape=jax.ShapeDtypeStruct((width, order) if partial is None else (order, width), jnp.float32),
        grid_spec=pltpu.PrefetchScalarGridSpec(
            num_scalar_prefetch=1,
            grid=(steps,),
            in_specs=[
                pl.BlockSpec((groups, 1, rows, chunk), lambda g, where: (0, where[0], 0, g)),
                pl.BlockSpec((groups, rows, width), lambda g, where: (0, 0, 0)),
            ]
            + ([] if partial is None else [flat]),
            out_specs=flat if partial is None else pl.BlockSpec((chunk, width), lambda g, where: (g, 0)),
            scratch_shapes=[
                pltpu.VMEM((depth, width), jnp.float32),
                pltpu.VMEM((2 * width, depth), jnp.bfloat16),
            ],
        ),
        compiler_params=pltpu.CompilerParams(vmem_limit_bytes=60 << 20),
        cost_estimate=kernel_cost(tile, width),
    )(jnp.concatenate([half[None], places]), tile, row_half, *([] if partial is None else [partial]))


def swap(value, axis, bit):
    size = lax.axis_size(axis)
    return lax.ppermute(value, axis, [(i, i ^ bit) for i in range(size)])


def bits_of(size):
    bit = size // 2
    while bit:
        yield bit
        bit //= 2


def relative_places(mine, groups):
    offset = jnp.arange(groups, dtype=jnp.int32) ^ mine
    count = groups.bit_length() - 1
    return sum(((offset >> k) & 1) << (count - 1 - k) for k in range(count))


def doubled(held, axis, bits):
    for bit in bits:
        held = jnp.concatenate([held, swap(held, axis, bit)], axis=0)
    return held


def halved(mine, got, axis):
    for bit in reversed(list(bits_of(lax.axis_size(axis)))):
        if bit > 1:
            half = mine.shape[0] // 2
            sent = mine[half:] + got[half:]
            mine, got = mine[:half] + got[:half], swap(sent, axis, bit)
    return mine[0] + got[0]


def apply_hamiltonian(tile, columns, vectors, want_gram):
    rows, width = vectors.shape
    count = lax.axis_size(NARROW)
    order = tile.shape[0]
    groups = count // 2
    me = lax.axis_index(NARROW).astype(jnp.int32)
    near, far = me & 1, (me & 1) ^ 1
    places = relative_places(me >> 1, groups)
    tile = tile.reshape(groups, 2, rows, order)
    with jax.named_scope("gather_wide"):
        slices = to_everyone(vectors, WIDE)
    bits = list(bits_of(groups))
    with jax.named_scope("gather_row"):
        near_rows = doubled(vectors[None], NARROW, [2 * bit for bit in bits])
        slices, near_rows = lax.optimization_barrier((slices, near_rows))
        far_rows = swap(near_rows, NARROW, 1)
    with jax.named_scope("gather_column"):
        picked = move_blocks(slices, columns, scatter=False)
        column_block = exchange(picked, NARROW).reshape(order, width)
    with jax.named_scope("transposed"):
        partial = transposed_half(tile, near_rows, near, places)
        transposed = transposed_half(tile, far_rows, far, places, partial)
    with jax.named_scope("back_transposed"):
        arrived = exchange(transposed.reshape(count, rows, width), NARROW)
    with jax.named_scope("direct"):
        sent = direct_half(tile, column_block, far, places)
        got = swap(sent, NARROW, 1)
        kept = direct_half(tile, column_block, near, places)
    gram = None
    if want_gram:
        with jax.named_scope("gram_block_row"):
            near_rows, far_rows, kept = lax.optimization_barrier((near_rows, far_rows, kept))
            gram = gram_of(near_rows.reshape(-1, width)) + gram_of(far_rows.reshape(-1, width))
    with jax.named_scope("back_direct"):
        direct_sum = halved(kept, got, NARROW)
    with jax.named_scope("back_wide"):
        placed = move_blocks(arrived, columns, scatter=True, extra=gram)
        sums = exchange(placed, WIDE).sum(axis=0)
    return direct_sum + sums[:rows], sums[rows:]


def exact(left, right):
    return jnp.dot(left, right, precision=HIGHEST, preferred_element_type=jnp.float32)


def inverse_root(gram, total_rows):
    width = gram.shape[0]
    row = lax.broadcasted_iota(jnp.int32, (width, width), 0)
    identity = (row == lax.broadcasted_iota(jnp.int32, (width, width), 1)).astype(jnp.float32)
    scale = jnp.sqrt(jnp.sum(gram * gram, keepdims=True) + 1e-06)
    current = gram / scale
    inverse = identity
    for repeat in range(NS_STEPS):
        middle = 1.5 * identity - 0.5 * exact(inverse, current)
        current = exact(current, middle)
        inverse = exact(middle, inverse)
    return inverse * jnp.sqrt(total_rows / scale)


def in_kernel(function, shape, *arrays):
    def kernel(*refs):
        refs[-1][...] = function(*(ref[...] for ref in refs[:-1]))

    return pl.pallas_call(
        kernel,
        out_shape=jax.ShapeDtypeStruct(shape, jnp.float32),
        cost_estimate=pl.CostEstimate(flops=1 << 30, bytes_accessed=1 << 20, transcendentals=0),
    )(*arrays)


def gram_of(value):
    return lax.dot_general(value, value, (((0,), (0,)), ((), ())), precision=HIGHEST)


def on_device(tile, row_columns, start_vectors):
    total_rows = float(lax.axis_size(WIDE) * lax.axis_size(NARROW) * start_vectors.shape[0])
    columns = row_columns[0]
    first, _ = apply_hamiltonian(tile, columns, start_vectors, want_gram=False)
    second, gram_rows = apply_hamiltonian(tile, columns, first, want_gram=True)
    width = second.shape[1]
    wide = lax.axis_size(WIDE)
    with jax.named_scope("gram_sum_wide"):
        parts = gram_of(second).reshape(wide, width // wide, width)
        given = jnp.broadcast_to(gram_rows[None], parts.shape)
        got = exchange(jnp.concatenate([parts, given], axis=1), WIDE)
        gram_second = got[:, : width // wide].sum(axis=0)
        gram_first = got[:, width // wide :].reshape(width, width)
    with jax.named_scope("gram_sum_narrow"):
        gram_second = to_everyone(gram_second, NARROW).sum(axis=0)
    with jax.named_scope("inverse_first"):
        root_first = in_kernel(lambda gram: inverse_root(gram, total_rows), (width, width), gram_first)
    with jax.named_scope("gram_whole"):
        gram_second = to_everyone(gram_second, WIDE).reshape(width, width)

    def finish(gram, root, value):
        gram = exact(root.T, exact(gram, root))
        return exact(exact(value, root), inverse_root(gram, total_rows))

    with jax.named_scope("finish"):
        return in_kernel(finish, second.shape, gram_second, root_first, second)


def solution(mesh):
    return jax.shard_map(
        on_device,
        mesh=mesh,
        in_specs=(P(WIDE, NARROW), P(WIDE, None), P((WIDE, NARROW), None)),
        out_specs=P((WIDE, NARROW), None),
        check_vma=False,
    )
```

```python
import jax
import jax.numpy as jnp
from jax import lax
from jax.experimental import pallas as pl
from jax.experimental.pallas import tpu as pltpu
from jax.sharding import PartitionSpec as P

NS_STEPS = 5
WIDE, NARROW = "wide", "narrow"
HIGHEST = lax.Precision.HIGHEST


def exchange(parts, axis):
    return lax.all_to_all(parts, axis, 0, 0, tiled=True)


def to_everyone(value, axis):
    return exchange(jnp.broadcast_to(value[None], (lax.axis_size(axis), *value.shape)), axis)


def move_blocks(blocks, columns, scatter, extra=None):
    count, rows, width = blocks.shape
    arrays = [blocks] if extra is None else [blocks, extra]
    more = 0 if extra is None else extra.shape[0] // count

    def kernel(columns_ref, blocks_ref, *rest):
        moved_ref, done = rest[-2:]
        copies = []
        for i in range(count):
            column = columns_ref[i]
            source, target = (i, column) if scatter else (column, i)
            copies.append(
                pltpu.make_async_copy(
                    blocks_ref.at[source], moved_ref.at[target, pl.ds(0, rows)], done.at[i]
                )
            )
            if more:
                copies.append(
                    pltpu.make_async_copy(
                        rest[0].at[pl.ds(i * more, more)],
                        moved_ref.at[i, pl.ds(rows, more)],
                        done.at[count + i],
                    )
                )
        for copy in copies:
            copy.start()
        for copy in copies:
            copy.wait()

    return pl.pallas_call(
        kernel,
        out_shape=jax.ShapeDtypeStruct((count, rows + more, width), blocks.dtype),
        in_specs=[pl.BlockSpec(memory_space=pltpu.SMEM)]
        + [pl.BlockSpec(memory_space=pl.ANY)] * len(arrays),
        out_specs=pl.BlockSpec(memory_space=pl.ANY),
        scratch_shapes=[pltpu.SemaphoreType.DMA((len(arrays) * count,))],
        compiler_params=pltpu.CompilerParams(vmem_limit_bytes=1 << 20),
        cost_estimate=pl.CostEstimate(flops=0, bytes_accessed=8 * blocks.size, transcendentals=0),
    )(columns, *arrays)


def high_low(value):
    high = value.astype(jnp.bfloat16)
    return high, (value - high.astype(jnp.float32)).astype(jnp.bfloat16)


def product_of(left, right):
    return jnp.dot(left, right, preferred_element_type=jnp.float32)


def kernel_cost(tile, width):
    return pl.CostEstimate(flops=3 * tile.size * width, bytes_accessed=2 * tile.size, transcendentals=0)


def direct_half(tile, column_block, half, places):
    groups, _, rows, order = tile.shape
    width = column_block.shape[1]
    steps = 2
    each = groups // steps

    def kernel(where_ref, tile_ref, column_ref, first_ref, second_ref, both):
        step = pl.program_id(0)

        @pl.when(step == 0)
        def _():
            high, low = high_low(column_ref[...])
            both[:, :width] = high
            both[:, width:] = low

        high, low = high_low(tile_ref[...].reshape(each * rows, order))
        wide = product_of(high, both[...])
        total = wide[:, :width] + wide[:, width:] + product_of(low, both[:, :width])
        for k in range(each):
            place = where_ref[1 + step * each + k]
            part = total[k * rows : (k + 1) * rows]

            @pl.when(place < each)
            def _():
                first_ref[place] = part

            @pl.when(place >= each)
            def _():
                second_ref[place - each] = part

    out = jax.ShapeDtypeStruct((each, rows, width), jnp.float32)
    return pl.pallas_call(
        kernel,
        out_shape=(out, out),
        grid_spec=pltpu.PrefetchScalarGridSpec(
            num_scalar_prefetch=1,
            grid=(steps,),
            in_specs=[
                pl.BlockSpec((each, 1, rows, order), lambda g, where: (g, where[0], 0, 0)),
                pl.BlockSpec((order, width), lambda g, where: (0, 0)),
            ],
            out_specs=[pl.BlockSpec((each, rows, width), lambda g, where: (0, 0, 0))] * 2,
            scratch_shapes=[pltpu.VMEM((order, 2 * width), jnp.bfloat16)],
        ),
        compiler_params=pltpu.CompilerParams(vmem_limit_bytes=60 << 20),
        cost_estimate=kernel_cost(tile, width),
    )(jnp.concatenate([half[None], places]), tile, column_block)


def transposed_half(tile, quarters, half, spots, partial=None):
    groups, _, rows, order = tile.shape
    width = quarters[0].shape[2]
    depth = groups * rows
    each = groups // 2
    steps = 3
    chunk = order // steps

    def kernel(where_ref, tile_ref, first_ref, second_ref, *rest):
        partial_ref, (out_ref, gathered, both) = (rest[0], rest[1:]) if partial is not None else (None, rest)

        @pl.when(pl.program_id(0) == 0)
        def _():
            for k in range(groups):
                spot = pl.multiple_of(where_ref[1 + k] * rows, rows)
                part = first_ref[k] if k < each else second_ref[k - each]
                gathered[pl.ds(spot, rows)] = part
            high, low = high_low(gathered[...].T)
            both[:width] = high
            both[width:] = low

        high, low = high_low(tile_ref[...].reshape(depth, chunk))
        wide = product_of(both[...], high)
        total = wide[:width] + wide[width:] + product_of(both[:width], low)
        if partial_ref is None:
            out_ref[...] = total
        else:
            out_ref[...] = (total + partial_ref[...]).T

    flat = pl.BlockSpec((width, chunk), lambda g, where: (0, g))
    return pl.pallas_call(
        kernel,
        out_shape=jax.ShapeDtypeStruct((width, order) if partial is None else (order, width), jnp.float32),
        grid_spec=pltpu.PrefetchScalarGridSpec(
            num_scalar_prefetch=1,
            grid=(steps,),
            in_specs=[
                pl.BlockSpec((groups, 1, rows, chunk), lambda g, where: (0, where[0], 0, g)),
            ]
            + [pl.BlockSpec((each, rows, width), lambda g, where: (0, 0, 0))] * 2
            + ([] if partial is None else [flat]),
            out_specs=flat if partial is None else pl.BlockSpec((chunk, width), lambda g, where: (g, 0)),
            scratch_shapes=[
                pltpu.VMEM((depth, width), jnp.float32),
                pltpu.VMEM((2 * width, depth), jnp.bfloat16),
            ],
        ),
        compiler_params=pltpu.CompilerParams(vmem_limit_bytes=60 << 20),
        cost_estimate=kernel_cost(tile, width),
    )(jnp.concatenate([half[None], spots]), tile, *quarters, *([] if partial is None else [partial]))


def swap(value, mask):
    size = lax.axis_size(NARROW)
    return lax.ppermute(value, NARROW, [(i, i ^ mask) for i in range(size)])


ENTRIES = (0, 8, 4, 12)
QUARTERS = (0, 2, 1, 3)
REVERSED = (0, 4, 2, 6, 1, 5, 3, 7)


def reversed_bits(value):
    return ((value & 1) << 2) | (value & 2) | (value >> 2)


def apply_hamiltonian(tile, columns, vectors, want_gram):
    rows, width = vectors.shape
    count = lax.axis_size(NARROW)
    order = tile.shape[0]
    groups = count // 2
    me = lax.axis_index(NARROW).astype(jnp.int32)
    near, far = me & 1, (me & 1) ^ 1
    table = jnp.array(REVERSED, jnp.int32)
    spots, places = table ^ (me >> 1), table ^ reversed_bits(me >> 1)
    tile = tile.reshape(groups, 2, rows, order)
    with jax.named_scope("gather_wide"):
        slices = to_everyone(vectors, WIDE)
    with jax.named_scope("gather_row"):
        quarter = jnp.stack([vectors] + [swap(vectors, mask) for mask in ENTRIES[1:]])
        quarters = [quarter] + [swap(quarter, mask) for mask in QUARTERS[1:]]
        slices, quarters = lax.optimization_barrier((slices, quarters))
    with jax.named_scope("gather_column"):
        picked = move_blocks(slices, columns, scatter=False)
        column_block = exchange(picked, NARROW).reshape(order, width)
    with jax.named_scope("transposed"):
        partial = transposed_half(tile, quarters[:2], near, spots)
        transposed = transposed_half(tile, quarters[2:], far, spots, partial)
        transposed, column_block = lax.optimization_barrier((transposed, column_block))
    with jax.named_scope("back_transposed"):
        arrived = exchange(transposed.reshape(count, rows, width), NARROW)
    with jax.named_scope("direct"):
        sums = list(direct_half(tile, column_block, far, places))
        got = [swap(value, mask) for value, mask in zip(sums, QUARTERS[2:])]
        kept, sent = direct_half(tile, column_block, near, places)
        arrived, got, kept, sent = lax.optimization_barrier((arrived, got, kept, sent))
        got.append(swap(sent, QUARTERS[1]))
    gram = None
    if want_gram:
        with jax.named_scope("gram_block_row"):
            quarters, _ = lax.optimization_barrier((quarters, sums))
            gram = sum(gram_of(quarter.reshape(-1, width)) for quarter in quarters)
    with jax.named_scope("back_direct"):
        kept = kept + got[0] + got[1] + got[2]
        direct_sum = kept[0]
        for m, mask in enumerate(ENTRIES[1:]):
            direct_sum = direct_sum + swap(kept[m + 1], mask)
    with jax.named_scope("back_wide"):
        placed = move_blocks(arrived, columns, scatter=True, extra=gram)
        sums = exchange(placed, WIDE).sum(axis=0)
    return direct_sum + sums[:rows], sums[rows:]


def exact(left, right):
    return jnp.dot(left, right, precision=HIGHEST, preferred_element_type=jnp.float32)


def inverse_root(gram, total_rows):
    width = gram.shape[0]
    row = lax.broadcasted_iota(jnp.int32, (width, width), 0)
    identity = (row == lax.broadcasted_iota(jnp.int32, (width, width), 1)).astype(jnp.float32)
    scale = jnp.sqrt(jnp.sum(gram * gram, keepdims=True) + 1e-06)
    current = gram / scale
    inverse = identity
    for repeat in range(NS_STEPS):
        middle = 1.5 * identity - 0.5 * exact(inverse, current)
        current = exact(current, middle)
        inverse = exact(middle, inverse)
    return inverse * jnp.sqrt(total_rows / scale)


def in_kernel(function, shape, *arrays):
    def kernel(*refs):
        refs[-1][...] = function(*(ref[...] for ref in refs[:-1]))

    return pl.pallas_call(
        kernel,
        out_shape=jax.ShapeDtypeStruct(shape, jnp.float32),
        cost_estimate=pl.CostEstimate(flops=1 << 30, bytes_accessed=1 << 20, transcendentals=0),
    )(*arrays)


def gram_of(value):
    return lax.dot_general(value, value, (((0,), (0,)), ((), ())), precision=HIGHEST)


def on_device(tile, row_columns, start_vectors):
    total_rows = float(lax.axis_size(WIDE) * lax.axis_size(NARROW) * start_vectors.shape[0])
    columns = row_columns[0]
    first, _ = apply_hamiltonian(tile, columns, start_vectors, want_gram=False)
    second, gram_rows = apply_hamiltonian(tile, columns, first, want_gram=True)
    width = second.shape[1]
    wide = lax.axis_size(WIDE)
    with jax.named_scope("gram_sum_wide"):
        parts = gram_of(second).reshape(wide, width // wide, width)
        given = jnp.broadcast_to(gram_rows[None], parts.shape)
        got = exchange(jnp.concatenate([parts, given], axis=1), WIDE)
        gram_second = got[:, : width // wide].sum(axis=0)
        gram_first = got[:, width // wide :].reshape(width, width)
    with jax.named_scope("gram_sum_narrow"):
        gram_second = to_everyone(gram_second, NARROW).sum(axis=0)
    with jax.named_scope("inverse_first"):
        root_first = in_kernel(lambda gram: inverse_root(gram, total_rows), (width, width), gram_first)
    with jax.named_scope("gram_whole"):
        gram_second = to_everyone(gram_second, WIDE).reshape(width, width)

    def finish(gram, root, value):
        gram = exact(root.T, exact(gram, root))
        return exact(exact(value, root), inverse_root(gram, total_rows))

    with jax.named_scope("finish"):
        return in_kernel(finish, second.shape, gram_second, root_first, second)


def solution(mesh):
    return jax.shard_map(
        on_device,
        mesh=mesh,
        in_specs=(P(WIDE, NARROW), P(WIDE, None), P((WIDE, NARROW), None)),
        out_specs=P((WIDE, NARROW), None),
        check_vma=False,
    )
```

```python
import jax
import jax.numpy as jnp
from jax import lax
from jax.experimental import pallas as pl
from jax.experimental.pallas import tpu as pltpu
from jax.sharding import PartitionSpec as P

NS_STEPS = 5
WIDE, NARROW = "wide", "narrow"
HIGHEST = lax.Precision.HIGHEST


def exchange(parts, axis):
    return lax.all_to_all(parts, axis, 0, 0, tiled=True)


def to_everyone(value, axis):
    return exchange(jnp.broadcast_to(value[None], (lax.axis_size(axis), *value.shape)), axis)


def move_blocks(blocks, columns, scatter, extra=None):
    count, rows, width = blocks.shape
    arrays = [blocks] if extra is None else [blocks, extra]
    more = 0 if extra is None else extra.shape[0] // count

    def kernel(columns_ref, blocks_ref, *rest):
        moved_ref, done = rest[-2:]
        copies = []
        for i in range(count):
            column = columns_ref[i]
            source, target = (i, column) if scatter else (column, i)
            copies.append(
                pltpu.make_async_copy(
                    blocks_ref.at[source], moved_ref.at[target, pl.ds(0, rows)], done.at[i]
                )
            )
            if more:
                copies.append(
                    pltpu.make_async_copy(
                        rest[0].at[pl.ds(i * more, more)],
                        moved_ref.at[i, pl.ds(rows, more)],
                        done.at[count + i],
                    )
                )
        for copy in copies:
            copy.start()
        for copy in copies:
            copy.wait()

    return pl.pallas_call(
        kernel,
        out_shape=jax.ShapeDtypeStruct((count, rows + more, width), blocks.dtype),
        in_specs=[pl.BlockSpec(memory_space=pltpu.SMEM)]
        + [pl.BlockSpec(memory_space=pl.ANY)] * len(arrays),
        out_specs=pl.BlockSpec(memory_space=pl.ANY),
        scratch_shapes=[pltpu.SemaphoreType.DMA((len(arrays) * count,))],
        compiler_params=pltpu.CompilerParams(vmem_limit_bytes=1 << 20),
        cost_estimate=pl.CostEstimate(flops=0, bytes_accessed=8 * blocks.size, transcendentals=0),
    )(columns, *arrays)


def high_low(value):
    high = value.astype(jnp.bfloat16)
    return high, (value - high.astype(jnp.float32)).astype(jnp.bfloat16)


def product_of(left, right):
    return jnp.dot(left, right, preferred_element_type=jnp.float32)


def kernel_cost(tile, width):
    return pl.CostEstimate(flops=3 * tile.size * width, bytes_accessed=2 * tile.size, transcendentals=0)


def split_tile(tile):
    block = pl.BlockSpec((1, *tile.shape[1:]), lambda g: (g, 0, 0, 0))

    def kernel(tile_ref, high_ref, low_ref):
        high_ref[...], low_ref[...] = high_low(tile_ref[...])

    out = jax.ShapeDtypeStruct(tile.shape, jnp.bfloat16)
    return pl.pallas_call(
        kernel,
        out_shape=(out, out),
        grid=(tile.shape[0],),
        in_specs=[block],
        out_specs=[block, block],
        compiler_params=pltpu.CompilerParams(vmem_limit_bytes=60 << 20),
        cost_estimate=pl.CostEstimate(flops=tile.size, bytes_accessed=8 * tile.size, transcendentals=0),
    )(tile)


def direct_half(tile, column_block, half, places):
    groups, _, rows, order = tile[0].shape
    width = column_block.shape[1]
    steps = 2
    each = groups // steps

    def kernel(where_ref, high_ref, low_ref, column_ref, out_ref, both):
        step = pl.program_id(0)

        @pl.when(step == 0)
        def _():
            high, low = high_low(column_ref[...])
            both[:, :width] = high
            both[:, width:] = low

        high, low = (ref[...].reshape(each * rows, order) for ref in (high_ref, low_ref))
        wide = product_of(high, both[...])
        total = wide[:, :width] + wide[:, width:] + product_of(low, both[:, :width])
        for k in range(each):
            out_ref[where_ref[1 + step * each + k]] = total[k * rows : (k + 1) * rows]

    return pl.pallas_call(
        kernel,
        out_shape=jax.ShapeDtypeStruct((groups, rows, width), jnp.float32),
        grid_spec=pltpu.PrefetchScalarGridSpec(
            num_scalar_prefetch=1,
            grid=(steps,),
            in_specs=[pl.BlockSpec((each, 1, rows, order), lambda g, where: (g, where[0], 0, 0))] * 2
            + [
                pl.BlockSpec((order, width), lambda g, where: (0, 0)),
            ],
            out_specs=pl.BlockSpec((groups, rows, width), lambda g, where: (0, 0, 0)),
            scratch_shapes=[pltpu.VMEM((order, 2 * width), jnp.bfloat16)],
        ),
        compiler_params=pltpu.CompilerParams(vmem_limit_bytes=60 << 20),
        cost_estimate=kernel_cost(tile[0], width),
    )(jnp.concatenate([half[None], places]), *tile, column_block)


def transposed_half(tile, row_half, half, places, partial=None):
    groups, _, rows, order = tile[0].shape
    width = row_half.shape[2]
    depth = groups * rows
    steps = 3
    chunk = order // steps

    def kernel(where_ref, high_ref, low_ref, row_ref, *rest):
        partial_ref, (out_ref, gathered, both) = (rest[0], rest[1:]) if partial is not None else (None, rest)

        @pl.when(pl.program_id(0) == 0)
        def _():
            for k in range(groups):
                gathered[k * rows : (k + 1) * rows] = row_ref[where_ref[1 + k]]
            high, low = high_low(gathered[...].T)
            both[:width] = high
            both[width:] = low

        high, low = (ref[...].reshape(depth, chunk) for ref in (high_ref, low_ref))
        wide = product_of(both[...], high)
        total = wide[:width] + wide[width:] + product_of(both[:width], low)
        if partial_ref is None:
            out_ref[...] = total
        else:
            out_ref[...] = (total + partial_ref[...]).T

    flat = pl.BlockSpec((width, chunk), lambda g, where: (0, g))
    return pl.pallas_call(
        kernel,
        out_shape=jax.ShapeDtypeStruct((width, order) if partial is None else (order, width), jnp.float32),
        grid_spec=pltpu.PrefetchScalarGridSpec(
            num_scalar_prefetch=1,
            grid=(steps,),
            in_specs=[pl.BlockSpec((groups, 1, rows, chunk), lambda g, where: (0, where[0], 0, g))] * 2
            + [
                pl.BlockSpec((groups, rows, width), lambda g, where: (0, 0, 0)),
            ]
            + ([] if partial is None else [flat]),
            out_specs=flat if partial is None else pl.BlockSpec((chunk, width), lambda g, where: (g, 0)),
            scratch_shapes=[
                pltpu.VMEM((depth, width), jnp.float32),
                pltpu.VMEM((2 * width, depth), jnp.bfloat16),
            ],
        ),
        compiler_params=pltpu.CompilerParams(vmem_limit_bytes=60 << 20),
        cost_estimate=kernel_cost(tile[0], width),
    )(jnp.concatenate([half[None], places]), *tile, row_half, *([] if partial is None else [partial]))


def swap(value, mask):
    size = lax.axis_size(NARROW)
    return lax.ppermute(value, NARROW, [(i, i ^ mask) for i in range(size)])


def relative_places(mine, groups):
    offset = jnp.arange(groups, dtype=jnp.int32) ^ mine
    count = groups.bit_length() - 1
    return sum(((offset >> k) & 1) << (count - 1 - k) for k in range(count))


ENTRIES = (8, 4, 12)


def gathered_half(value):
    quarter = jnp.stack([value] + [swap(value, mask) for mask in ENTRIES])
    return jnp.concatenate([quarter, swap(quarter, 2)], axis=0)


def kept_half(kept, got):
    half = kept.shape[0] // 2
    sent = kept[half:] + got[half:]
    return kept[:half] + got[:half] + swap(sent, 2)


def summed_part(kept):
    total = kept[0]
    for k, mask in enumerate(ENTRIES):
        total = total + swap(kept[k + 1], mask)
    return total


def apply_hamiltonian(tile, columns, vectors, want_gram):
    rows, width = vectors.shape
    count = lax.axis_size(NARROW)
    order = count * rows
    groups = count // 2
    me = lax.axis_index(NARROW).astype(jnp.int32)
    near, far = me & 1, (me & 1) ^ 1
    places = relative_places(me >> 1, groups)
    with jax.named_scope("gather_wide"):
        slices = to_everyone(vectors, WIDE)
    with jax.named_scope("gather_row"):
        near_rows = gathered_half(vectors)
        slices, near_rows = lax.optimization_barrier((slices, near_rows))
        far_rows = swap(near_rows, 1)
    with jax.named_scope("gather_column"):
        picked = move_blocks(slices, columns, scatter=False)
        column_block = exchange(picked, NARROW).reshape(order, width)
    if not isinstance(tile, (list, tuple)):
        with jax.named_scope("split_tile"):
            tile, near_rows = lax.optimization_barrier((tile, near_rows))
            tile = split_tile(tile.reshape(groups, 2, rows, order))
    with jax.named_scope("transposed"):
        partial = transposed_half(tile, near_rows, near, places)
        transposed = transposed_half(tile, far_rows, far, places, partial)
        transposed, column_block = lax.optimization_barrier((transposed, column_block))
    with jax.named_scope("back_transposed"):
        arrived = exchange(transposed.reshape(count, rows, width), NARROW)
    with jax.named_scope("direct"):
        sent = direct_half(tile, column_block, far, places)
        got = swap(sent, 1)
        kept = direct_half(tile, column_block, near, places)
        kept = kept_half(kept, got)
        arrived, kept = lax.optimization_barrier((arrived, kept))
    gram = None
    if want_gram:
        with jax.named_scope("gram_block_row"):
            near_rows, far_rows, _ = lax.optimization_barrier((near_rows, far_rows, sent))
            gram = gram_of(near_rows.reshape(-1, width)) + gram_of(far_rows.reshape(-1, width))
    with jax.named_scope("back_direct"):
        direct_sum = summed_part(kept)
    with jax.named_scope("back_wide"):
        placed = move_blocks(arrived, columns, scatter=True, extra=gram)
        sums = exchange(placed, WIDE).sum(axis=0)
    return direct_sum + sums[:rows], sums[rows:], tile


def exact(left, right):
    return jnp.dot(left, right, precision=HIGHEST, preferred_element_type=jnp.float32)


def inverse_root(gram, total_rows):
    width = gram.shape[0]
    row = lax.broadcasted_iota(jnp.int32, (width, width), 0)
    identity = (row == lax.broadcasted_iota(jnp.int32, (width, width), 1)).astype(jnp.float32)
    scale = jnp.sqrt(jnp.sum(gram * gram, keepdims=True) + 1e-06)
    current = gram / scale
    inverse = identity
    for repeat in range(NS_STEPS):
        middle = 1.5 * identity - 0.5 * exact(inverse, current)
        current = exact(current, middle)
        inverse = exact(middle, inverse)
    return inverse * jnp.sqrt(total_rows / scale)


def in_kernel(function, shape, *arrays):
    def kernel(*refs):
        refs[-1][...] = function(*(ref[...] for ref in refs[:-1]))

    return pl.pallas_call(
        kernel,
        out_shape=jax.ShapeDtypeStruct(shape, jnp.float32),
        cost_estimate=pl.CostEstimate(flops=1 << 30, bytes_accessed=1 << 20, transcendentals=0),
    )(*arrays)


def gram_of(value):
    return lax.dot_general(value, value, (((0,), (0,)), ((), ())), precision=HIGHEST)


def on_device(tile, row_columns, start_vectors):
    total_rows = float(lax.axis_size(WIDE) * lax.axis_size(NARROW) * start_vectors.shape[0])
    columns = row_columns[0]
    first, _, tile = apply_hamiltonian(tile, columns, start_vectors, want_gram=False)
    second, gram_rows, _ = apply_hamiltonian(tile, columns, first, want_gram=True)
    width = second.shape[1]
    wide = lax.axis_size(WIDE)
    with jax.named_scope("gram_sum_wide"):
        parts = gram_of(second).reshape(wide, width // wide, width)
        given = jnp.broadcast_to(gram_rows[None], parts.shape)
        got = exchange(jnp.concatenate([parts, given], axis=1), WIDE)
        gram_second = got[:, : width // wide].sum(axis=0)
        gram_first = got[:, width // wide :].reshape(width, width)
    with jax.named_scope("gram_sum_narrow"):
        gram_second = to_everyone(gram_second, NARROW).sum(axis=0)
    with jax.named_scope("inverse_first"):
        root_first = in_kernel(lambda gram: inverse_root(gram, total_rows), (width, width), gram_first)
    with jax.named_scope("gram_whole"):
        gram_second = to_everyone(gram_second, WIDE).reshape(width, width)

    def finish(gram, root, value):
        gram = exact(root.T, exact(gram, root))
        return exact(exact(value, root), inverse_root(gram, total_rows))

    with jax.named_scope("finish"):
        return in_kernel(finish, second.shape, gram_second, root_first, second)


def solution(mesh):
    return jax.shard_map(
        on_device,
        mesh=mesh,
        in_specs=(P(WIDE, NARROW), P(WIDE, None), P((WIDE, NARROW), None)),
        out_specs=P((WIDE, NARROW), None),
        check_vma=False,
    )
```

```python
import jax
import jax.numpy as jnp
from jax import lax
from jax.experimental import pallas as pl
from jax.experimental.pallas import tpu as pltpu
from jax.sharding import PartitionSpec as P

NS_STEPS = 5
WIDE, NARROW = "wide", "narrow"
HIGHEST = lax.Precision.HIGHEST


def exchange(parts, axis):
    return lax.all_to_all(parts, axis, 0, 0, tiled=True)


def to_everyone(value, axis):
    return exchange(jnp.broadcast_to(value[None], (lax.axis_size(axis), *value.shape)), axis)


def move_blocks(blocks, columns, scatter, extra=None):
    count, rows, width = blocks.shape
    arrays = [blocks] if extra is None else [blocks, extra]
    more = 0 if extra is None else extra.shape[0] // count

    def kernel(columns_ref, blocks_ref, *rest):
        moved_ref, done = rest[-2:]
        copies = []
        for i in range(count):
            column = columns_ref[i]
            source, target = (i, column) if scatter else (column, i)
            copies.append(
                pltpu.make_async_copy(
                    blocks_ref.at[source], moved_ref.at[target, pl.ds(0, rows)], done.at[i]
                )
            )
            if more:
                copies.append(
                    pltpu.make_async_copy(
                        rest[0].at[pl.ds(i * more, more)],
                        moved_ref.at[i, pl.ds(rows, more)],
                        done.at[count + i],
                    )
                )
        for copy in copies:
            copy.start()
        for copy in copies:
            copy.wait()

    return pl.pallas_call(
        kernel,
        out_shape=jax.ShapeDtypeStruct((count, rows + more, width), blocks.dtype),
        in_specs=[pl.BlockSpec(memory_space=pltpu.SMEM)]
        + [pl.BlockSpec(memory_space=pl.ANY)] * len(arrays),
        out_specs=pl.BlockSpec(memory_space=pl.ANY),
        scratch_shapes=[pltpu.SemaphoreType.DMA((len(arrays) * count,))],
        compiler_params=pltpu.CompilerParams(vmem_limit_bytes=1 << 20),
        cost_estimate=pl.CostEstimate(flops=0, bytes_accessed=8 * blocks.size, transcendentals=0),
    )(columns, *arrays)


def high_low(value):
    high = value.astype(jnp.bfloat16)
    return high, (value - high.astype(jnp.float32)).astype(jnp.bfloat16)


def product_of(left, right):
    return jnp.dot(left, right, preferred_element_type=jnp.float32)


def kernel_cost(tile, width):
    return pl.CostEstimate(flops=3 * tile.size * width, bytes_accessed=2 * tile.size, transcendentals=0)


def direct_half(tile, column_block, half, places):
    groups, _, rows, order = tile.shape
    width = column_block.shape[1]
    steps = 2
    each = groups // steps

    def kernel(where_ref, tile_ref, column_ref, first_ref, second_ref, both):
        step = pl.program_id(0)

        @pl.when(step == 0)
        def _():
            high, low = high_low(column_ref[...])
            both[:, :width] = high
            both[:, width:] = low

        high, low = high_low(tile_ref[...].reshape(each * rows, order))
        wide = product_of(high, both[...])
        total = wide[:, :width] + wide[:, width:] + product_of(low, both[:, :width])
        for k in range(each):
            place = where_ref[1 + step * each + k]
            part = total[k * rows : (k + 1) * rows]

            @pl.when(place < each)
            def _():
                first_ref[place] = part

            @pl.when(place >= each)
            def _():
                second_ref[place - each] = part

    out = jax.ShapeDtypeStruct((each, rows, width), jnp.float32)
    return pl.pallas_call(
        kernel,
        out_shape=(out, out),
        grid_spec=pltpu.PrefetchScalarGridSpec(
            num_scalar_prefetch=1,
            grid=(steps,),
            in_specs=[
                pl.BlockSpec((each, 1, rows, order), lambda g, where: (g, where[0], 0, 0)),
                pl.BlockSpec((order, width), lambda g, where: (0, 0)),
            ],
            out_specs=[pl.BlockSpec((each, rows, width), lambda g, where: (0, 0, 0))] * 2,
            scratch_shapes=[pltpu.VMEM((order, 2 * width), jnp.bfloat16)],
        ),
        compiler_params=pltpu.CompilerParams(vmem_limit_bytes=60 << 20),
        cost_estimate=kernel_cost(tile, width),
    )(jnp.concatenate([half[None], places]), tile, column_block)


def transposed_half(tile, quarters, half, spots, partial=None):
    groups, _, rows, order = tile.shape
    width = quarters[0].shape[2]
    depth = groups * rows
    each = groups // 2
    steps = 3
    chunk = order // steps

    def kernel(where_ref, tile_ref, first_ref, second_ref, *rest):
        partial_ref, (out_ref, gathered, both) = (rest[0], rest[1:]) if partial is not None else (None, rest)

        @pl.when(pl.program_id(0) == 0)
        def _():
            for k in range(groups):
                spot = pl.multiple_of(where_ref[1 + k] * rows, rows)
                part = first_ref[k] if k < each else second_ref[k - each]
                gathered[pl.ds(spot, rows)] = part
            high, low = high_low(gathered[...].T)
            both[:width] = high
            both[width:] = low

        high, low = high_low(tile_ref[...].reshape(depth, chunk))
        wide = product_of(both[...], high)
        total = wide[:width] + wide[width:] + product_of(both[:width], low)
        if partial_ref is None:
            out_ref[...] = total
        else:
            out_ref[...] = (total + partial_ref[...]).T

    flat = pl.BlockSpec((width, chunk), lambda g, where: (0, g))
    return pl.pallas_call(
        kernel,
        out_shape=jax.ShapeDtypeStruct((width, order) if partial is None else (order, width), jnp.float32),
        grid_spec=pltpu.PrefetchScalarGridSpec(
            num_scalar_prefetch=1,
            grid=(steps,),
            in_specs=[
                pl.BlockSpec((groups, 1, rows, chunk), lambda g, where: (0, where[0], 0, g)),
            ]
            + [pl.BlockSpec((each, rows, width), lambda g, where: (0, 0, 0))] * 2
            + ([] if partial is None else [flat]),
            out_specs=flat if partial is None else pl.BlockSpec((chunk, width), lambda g, where: (g, 0)),
            scratch_shapes=[
                pltpu.VMEM((depth, width), jnp.float32),
                pltpu.VMEM((2 * width, depth), jnp.bfloat16),
            ],
        ),
        compiler_params=pltpu.CompilerParams(vmem_limit_bytes=60 << 20),
        cost_estimate=kernel_cost(tile, width),
    )(jnp.concatenate([half[None], spots]), tile, *quarters, *([] if partial is None else [partial]))


def swap(value, mask):
    size = lax.axis_size(NARROW)
    return lax.ppermute(value, NARROW, [(i, i ^ mask) for i in range(size)])


ENTRIES = (8, 4, 12)
REVERSED = (0, 4, 2, 6, 1, 5, 3, 7)


def reversed_bits(value):
    return ((value & 1) << 2) | (value & 2) | (value >> 2)


def summed_part(kept):
    total = kept[0]
    for k, mask in enumerate(ENTRIES):
        total = total + swap(kept[k + 1], mask)
    return total


def apply_hamiltonian(tile, columns, vectors, want_gram):
    rows, width = vectors.shape
    count = lax.axis_size(NARROW)
    order = count * rows
    groups = count // 2
    me = lax.axis_index(NARROW).astype(jnp.int32)
    near, far = me & 1, (me & 1) ^ 1
    table = jnp.array(REVERSED, jnp.int32)
    spots, places = table ^ (me >> 1), table ^ reversed_bits(me >> 1)
    tile = tile.reshape(groups, 2, rows, order)
    with jax.named_scope("gather_wide"):
        slices = to_everyone(vectors, WIDE)
    with jax.named_scope("gather_row"):
        quarter = jnp.stack([vectors] + [swap(vectors, mask) for mask in ENTRIES])
        near_rows, far_rows = [quarter, swap(quarter, 2)], [swap(quarter, 1)]
        slices, near_rows, far_rows = lax.optimization_barrier((slices, near_rows, far_rows))
        far_rows.append(swap(near_rows[1], 1))
    with jax.named_scope("gather_column"):
        picked = move_blocks(slices, columns, scatter=False)
        column_block = exchange(picked, NARROW).reshape(order, width)
    with jax.named_scope("transposed"):
        partial = transposed_half(tile, near_rows, near, spots)
        transposed = transposed_half(tile, far_rows, far, spots, partial)
        transposed, column_block = lax.optimization_barrier((transposed, column_block))
    with jax.named_scope("back_transposed"):
        arrived = exchange(transposed.reshape(count, rows, width), NARROW)
    with jax.named_scope("direct"):
        far_first, far_second = direct_half(tile, column_block, far, places)
        got_second, got_first = swap(far_second, 1), swap(far_first, 1)
        near_first, near_second = direct_half(tile, column_block, near, places)
        kept = near_first + got_first + swap(near_second + got_second, 2)
        arrived, kept = lax.optimization_barrier((arrived, kept))
    gram = None
    if want_gram:
        with jax.named_scope("gram_block_row"):
            block, _ = lax.optimization_barrier((near_rows + far_rows, far_first))
            gram = sum(gram_of(quarter.reshape(-1, width)) for quarter in block)
    with jax.named_scope("back_direct"):
        direct_sum = summed_part(kept)
    with jax.named_scope("back_wide"):
        placed = move_blocks(arrived, columns, scatter=True, extra=gram)
        sums = exchange(placed, WIDE).sum(axis=0)
    return direct_sum + sums[:rows], sums[rows:]


def exact(left, right):
    return jnp.dot(left, right, precision=HIGHEST, preferred_element_type=jnp.float32)


def inverse_root(gram, total_rows):
    width = gram.shape[0]
    row = lax.broadcasted_iota(jnp.int32, (width, width), 0)
    identity = (row == lax.broadcasted_iota(jnp.int32, (width, width), 1)).astype(jnp.float32)
    scale = jnp.sqrt(jnp.sum(gram * gram, keepdims=True) + 1e-06)
    current = gram / scale
    inverse = identity
    for repeat in range(NS_STEPS):
        middle = 1.5 * identity - 0.5 * exact(inverse, current)
        current = exact(current, middle)
        inverse = exact(middle, inverse)
    return inverse * jnp.sqrt(total_rows / scale)


def in_kernel(function, shape, *arrays):
    def kernel(*refs):
        refs[-1][...] = function(*(ref[...] for ref in refs[:-1]))

    return pl.pallas_call(
        kernel,
        out_shape=jax.ShapeDtypeStruct(shape, jnp.float32),
        cost_estimate=pl.CostEstimate(flops=1 << 30, bytes_accessed=1 << 20, transcendentals=0),
    )(*arrays)


def gram_of(value):
    return lax.dot_general(value, value, (((0,), (0,)), ((), ())), precision=HIGHEST)


def on_device(tile, row_columns, start_vectors):
    total_rows = float(lax.axis_size(WIDE) * lax.axis_size(NARROW) * start_vectors.shape[0])
    columns = row_columns[0]
    first, _ = apply_hamiltonian(tile, columns, start_vectors, want_gram=False)
    second, gram_rows = apply_hamiltonian(tile, columns, first, want_gram=True)
    width = second.shape[1]
    wide = lax.axis_size(WIDE)
    with jax.named_scope("gram_sum_wide"):
        parts = gram_of(second).reshape(wide, width // wide, width)
        given = jnp.broadcast_to(gram_rows[None], parts.shape)
        got = exchange(jnp.concatenate([parts, given], axis=1), WIDE)
        gram_second = got[:, : width // wide].sum(axis=0)
        gram_first = got[:, width // wide :].reshape(width, width)
    with jax.named_scope("gram_sum_narrow"):
        gram_second = to_everyone(gram_second, NARROW).sum(axis=0)
    with jax.named_scope("inverse_first"):
        root_first = in_kernel(lambda gram: inverse_root(gram, total_rows), (width, width), gram_first)
    with jax.named_scope("gram_whole"):
        gram_second = to_everyone(gram_second, WIDE).reshape(width, width)

    def finish(gram, root, value):
        gram = exact(root.T, exact(gram, root))
        return exact(exact(value, root), inverse_root(gram, total_rows))

    with jax.named_scope("finish"):
        return in_kernel(finish, second.shape, gram_second, root_first, second)


def solution(mesh):
    return jax.shard_map(
        on_device,
        mesh=mesh,
        in_specs=(P(WIDE, NARROW), P(WIDE, None), P((WIDE, NARROW), None)),
        out_specs=P((WIDE, NARROW), None),
        check_vma=False,
    )
```

```python
import jax
import jax.numpy as jnp
from jax import lax
from jax.experimental import pallas as pl
from jax.experimental.pallas import tpu as pltpu
from jax.sharding import PartitionSpec as P

NS_STEPS = 5
WIDE, NARROW = "wide", "narrow"
HIGHEST = lax.Precision.HIGHEST


def exchange(parts, axis):
    return lax.all_to_all(parts, axis, 0, 0, tiled=True)


def to_everyone(value, axis):
    return exchange(jnp.broadcast_to(value[None], (lax.axis_size(axis), *value.shape)), axis)


def move_blocks(blocks, columns, scatter, extra=None):
    count, rows, width = blocks.shape
    arrays = [blocks] if extra is None else [blocks, extra]
    more = 0 if extra is None else extra.shape[0] // count

    def kernel(columns_ref, blocks_ref, *rest):
        moved_ref, done = rest[-2:]
        copies = []
        for i in range(count):
            column = columns_ref[i]
            source, target = (i, column) if scatter else (column, i)
            copies.append(
                pltpu.make_async_copy(
                    blocks_ref.at[source], moved_ref.at[target, pl.ds(0, rows)], done.at[i]
                )
            )
            if more:
                copies.append(
                    pltpu.make_async_copy(
                        rest[0].at[pl.ds(i * more, more)],
                        moved_ref.at[i, pl.ds(rows, more)],
                        done.at[count + i],
                    )
                )
        for copy in copies:
            copy.start()
        for copy in copies:
            copy.wait()

    return pl.pallas_call(
        kernel,
        out_shape=jax.ShapeDtypeStruct((count, rows + more, width), blocks.dtype),
        in_specs=[pl.BlockSpec(memory_space=pltpu.SMEM)]
        + [pl.BlockSpec(memory_space=pl.ANY)] * len(arrays),
        out_specs=pl.BlockSpec(memory_space=pl.ANY),
        scratch_shapes=[pltpu.SemaphoreType.DMA((len(arrays) * count,))],
        compiler_params=pltpu.CompilerParams(vmem_limit_bytes=1 << 20),
        cost_estimate=pl.CostEstimate(flops=0, bytes_accessed=8 * blocks.size, transcendentals=0),
    )(columns, *arrays)


def high_low(value):
    high = value.astype(jnp.bfloat16)
    return high, (value - high.astype(jnp.float32)).astype(jnp.bfloat16)


def product_of(left, right):
    return jnp.dot(left, right, preferred_element_type=jnp.float32)


def kernel_cost(tile, width):
    return pl.CostEstimate(flops=3 * tile.size * width, bytes_accessed=2 * tile.size, transcendentals=0)


def direct_quarters(tile, column_block, quarters, places):
    each, _, _, rows, order = tile.shape
    width = column_block.shape[1]
    steps = len(quarters)

    def kernel(where_ref, tile_ref, column_ref, *rest):
        out_refs, both = rest[:-1], rest[-1]
        step = pl.program_id(0)

        @pl.when(step == 0)
        def _():
            high, low = high_low(column_ref[...])
            both[:, :width] = high
            both[:, width:] = low

        high, low = high_low(tile_ref[...].reshape(each * rows, order))
        wide = product_of(high, both[...])
        total = wide[:, :width] + wide[:, width:] + product_of(low, both[:, :width])
        for g, out_ref in enumerate(out_refs):

            @pl.when(step == g)
            def _():
                for k in range(each):
                    out_ref[where_ref[2 * steps + k]] = total[k * rows : (k + 1) * rows]

    return pl.pallas_call(
        kernel,
        out_shape=[jax.ShapeDtypeStruct((each, rows, width), jnp.float32)] * steps,
        grid_spec=pltpu.PrefetchScalarGridSpec(
            num_scalar_prefetch=1,
            grid=(steps,),
            in_specs=[
                pl.BlockSpec(
                    (each, 1, 1, rows, order), lambda g, where: (0, where[2 * g], where[2 * g + 1], 0, 0)
                ),
                pl.BlockSpec((order, width), lambda g, where: (0, 0)),
            ],
            out_specs=[pl.BlockSpec((each, rows, width), lambda g, where: (0, 0, 0))] * steps,
            scratch_shapes=[pltpu.VMEM((order, 2 * width), jnp.bfloat16)],
        ),
        compiler_params=pltpu.CompilerParams(vmem_limit_bytes=60 << 20),
        cost_estimate=pl.CostEstimate(
            flops=3 * steps * each * rows * order * width,
            bytes_accessed=4 * steps * each * rows * order,
            transcendentals=0,
        ),
    )(jnp.concatenate([jnp.stack([bit for pair in quarters for bit in pair]), places]), tile, column_block)


def transposed_half(tile, quarters, half, spots, partial=None):
    groups, _, rows, order = tile.shape
    width = quarters[0].shape[2]
    depth = groups * rows
    each = groups // 2
    steps = 3
    chunk = order // steps

    def kernel(where_ref, tile_ref, first_ref, second_ref, *rest):
        partial_ref, (out_ref, gathered, both) = (rest[0], rest[1:]) if partial is not None else (None, rest)

        @pl.when(pl.program_id(0) == 0)
        def _():
            for k in range(groups):
                spot = pl.multiple_of(where_ref[1 + k] * rows, rows)
                part = first_ref[k] if k < each else second_ref[k - each]
                gathered[pl.ds(spot, rows)] = part
            high, low = high_low(gathered[...].T)
            both[:width] = high
            both[width:] = low

        high, low = high_low(tile_ref[...].reshape(depth, chunk))
        wide = product_of(both[...], high)
        total = wide[:width] + wide[width:] + product_of(both[:width], low)
        if partial_ref is None:
            out_ref[...] = total
        else:
            out_ref[...] = (total + partial_ref[...]).T

    flat = pl.BlockSpec((width, chunk), lambda g, where: (0, g))
    return pl.pallas_call(
        kernel,
        out_shape=jax.ShapeDtypeStruct((width, order) if partial is None else (order, width), jnp.float32),
        grid_spec=pltpu.PrefetchScalarGridSpec(
            num_scalar_prefetch=1,
            grid=(steps,),
            in_specs=[
                pl.BlockSpec((groups, 1, rows, chunk), lambda g, where: (0, where[0], 0, g)),
            ]
            + [pl.BlockSpec((each, rows, width), lambda g, where: (0, 0, 0))] * 2
            + ([] if partial is None else [flat]),
            out_specs=flat if partial is None else pl.BlockSpec((chunk, width), lambda g, where: (g, 0)),
            scratch_shapes=[
                pltpu.VMEM((depth, width), jnp.float32),
                pltpu.VMEM((2 * width, depth), jnp.bfloat16),
            ],
        ),
        compiler_params=pltpu.CompilerParams(vmem_limit_bytes=60 << 20),
        cost_estimate=kernel_cost(tile, width),
    )(jnp.concatenate([half[None], spots]), tile, *quarters, *([] if partial is None else [partial]))


def swap(value, mask):
    size = lax.axis_size(NARROW)
    return lax.ppermute(value, NARROW, [(i, i ^ mask) for i in range(size)])


ENTRIES = (8, 4, 12)
REVERSED = (0, 4, 2, 6, 1, 5, 3, 7)
REVERSED_PAIR = (0, 2, 1, 3)


def summed_part(kept):
    total = kept[0]
    for k, mask in enumerate(ENTRIES):
        total = total + swap(kept[k + 1], mask)
    return total


def apply_hamiltonian(tile, columns, vectors, want_gram):
    rows, width = vectors.shape
    count = lax.axis_size(NARROW)
    order = count * rows
    groups = count // 2
    me = lax.axis_index(NARROW).astype(jnp.int32)
    near, far = me & 1, (me & 1) ^ 1
    table = jnp.array(REVERSED, jnp.int32)
    spots = table ^ (me >> 1)
    tile = tile.reshape(groups, 2, rows, order)
    with jax.named_scope("gather_wide"):
        slices = to_everyone(vectors, WIDE)
    with jax.named_scope("gather_row"):
        quarter = jnp.stack([vectors] + [swap(vectors, mask) for mask in ENTRIES])
        near_rows, far_rows = [quarter, swap(quarter, 2)], [swap(quarter, 1)]
        slices, near_rows, far_rows = lax.optimization_barrier((slices, near_rows, far_rows))
        far_rows.append(swap(near_rows[1], 1))
    with jax.named_scope("gather_column"):
        picked = move_blocks(slices, columns, scatter=False)
        column_block = exchange(picked, NARROW).reshape(order, width)
    with jax.named_scope("transposed"):
        partial = transposed_half(tile, near_rows, near, spots)
        transposed = transposed_half(tile, far_rows, far, spots, partial)
        transposed, column_block = lax.optimization_barrier((transposed, column_block))
    with jax.named_scope("back_transposed"):
        arrived = exchange(transposed.reshape(count, rows, width), NARROW)
    with jax.named_scope("direct"):
        quarters = tile.reshape(groups // 2, 2, 2, rows, order)
        first, second = (me >> 1) & 1, ((me >> 1) & 1) ^ 1
        high_bits = me >> 2
        places = jnp.array(REVERSED_PAIR, jnp.int32) ^ ((high_bits & 1) << 1 | high_bits >> 1)
        (far_second,) = direct_quarters(quarters, column_block, [(second, far)], places)
        column_block, far_second = lax.optimization_barrier((column_block, far_second))
        got_second = swap(far_second, 1)
        far_first, near_second = direct_quarters(
            quarters, column_block, [(first, far), (second, near)], places
        )
        column_block, far_first = lax.optimization_barrier((column_block, far_first))
        got_first = swap(far_first, 1)
        (near_first,) = direct_quarters(quarters, column_block, [(first, near)], places)
        kept = near_first + got_first + swap(near_second + got_second, 2)
        arrived, kept = lax.optimization_barrier((arrived, kept))
    gram = None
    if want_gram:
        with jax.named_scope("gram_block_row"):
            block, _ = lax.optimization_barrier((near_rows + far_rows, near_first))
            gram = sum(gram_of(quarter.reshape(-1, width)) for quarter in block)
    with jax.named_scope("back_direct"):
        direct_sum = summed_part(kept)
    with jax.named_scope("back_wide"):
        placed = move_blocks(arrived, columns, scatter=True, extra=gram)
        sums = exchange(placed, WIDE).sum(axis=0)
    return direct_sum + sums[:rows], sums[rows:]


def exact(left, right):
    return jnp.dot(left, right, precision=HIGHEST, preferred_element_type=jnp.float32)


def inverse_root(gram, total_rows):
    width = gram.shape[0]
    row = lax.broadcasted_iota(jnp.int32, (width, width), 0)
    identity = (row == lax.broadcasted_iota(jnp.int32, (width, width), 1)).astype(jnp.float32)
    scale = jnp.sqrt(jnp.sum(gram * gram, keepdims=True) + 1e-06)
    current = gram / scale
    inverse = identity
    for repeat in range(NS_STEPS):
        middle = 1.5 * identity - 0.5 * exact(inverse, current)
        current = exact(current, middle)
        inverse = exact(middle, inverse)
    return inverse * jnp.sqrt(total_rows / scale)


def in_kernel(function, shape, *arrays):
    def kernel(*refs):
        refs[-1][...] = function(*(ref[...] for ref in refs[:-1]))

    return pl.pallas_call(
        kernel,
        out_shape=jax.ShapeDtypeStruct(shape, jnp.float32),
        cost_estimate=pl.CostEstimate(flops=1 << 30, bytes_accessed=1 << 20, transcendentals=0),
    )(*arrays)


def gram_of(value):
    return lax.dot_general(value, value, (((0,), (0,)), ((), ())), precision=HIGHEST)


def on_device(tile, row_columns, start_vectors):
    total_rows = float(lax.axis_size(WIDE) * lax.axis_size(NARROW) * start_vectors.shape[0])
    columns = row_columns[0]
    first, _ = apply_hamiltonian(tile, columns, start_vectors, want_gram=False)
    second, gram_rows = apply_hamiltonian(tile, columns, first, want_gram=True)
    width = second.shape[1]
    wide = lax.axis_size(WIDE)
    with jax.named_scope("gram_sum_wide"):
        parts = gram_of(second).reshape(wide, width // wide, width)
        given = jnp.broadcast_to(gram_rows[None], parts.shape)
        got = exchange(jnp.concatenate([parts, given], axis=1), WIDE)
        gram_second = got[:, : width // wide].sum(axis=0)
        gram_first = got[:, width // wide :].reshape(width, width)
    with jax.named_scope("gram_sum_narrow"):
        gram_second = to_everyone(gram_second, NARROW).sum(axis=0)
    with jax.named_scope("inverse_first"):
        root_first = in_kernel(lambda gram: inverse_root(gram, total_rows), (width, width), gram_first)
    with jax.named_scope("gram_whole"):
        gram_second = to_everyone(gram_second, WIDE).reshape(width, width)

    def finish(gram, root, value):
        gram = exact(root.T, exact(gram, root))
        return exact(exact(value, root), inverse_root(gram, total_rows))

    with jax.named_scope("finish"):
        return in_kernel(finish, second.shape, gram_second, root_first, second)


def solution(mesh):
    return jax.shard_map(
        on_device,
        mesh=mesh,
        in_specs=(P(WIDE, NARROW), P(WIDE, None), P((WIDE, NARROW), None)),
        out_specs=P((WIDE, NARROW), None),
        check_vma=False,
    )
```

```python
import jax
import jax.numpy as jnp
from jax import lax
from jax.experimental import pallas as pl
from jax.experimental.pallas import tpu as pltpu
from jax.sharding import Mesh
from jax.sharding import PartitionSpec as P

NS_STEPS = 5
CHIP, CORE, NARROW = "chip", "core", "narrow"
WIDE = (CHIP, CORE)
HIGHEST = lax.Precision.HIGHEST


def exchange(parts, axis):
    return lax.all_to_all(parts, axis, 0, 0, tiled=True)


def to_everyone(value, axis):
    return exchange(jnp.broadcast_to(value[None], (lax.axis_size(axis), *value.shape)), axis)


def picked_blocks(blocks, columns):
    count = blocks.shape[0]

    def kernel(columns_ref, blocks_ref, picked_ref, done):
        copies = [
            pltpu.make_async_copy(blocks_ref.at[columns_ref[i]], picked_ref.at[i], done.at[i])
            for i in range(count)
        ]
        for copy in copies:
            copy.start()
        for copy in copies:
            copy.wait()

    return pl.pallas_call(
        kernel,
        out_shape=jax.ShapeDtypeStruct(blocks.shape, blocks.dtype),
        in_specs=[pl.BlockSpec(memory_space=pltpu.SMEM), pl.BlockSpec(memory_space=pl.ANY)],
        out_specs=pl.BlockSpec(memory_space=pl.ANY),
        scratch_shapes=[pltpu.SemaphoreType.DMA((count,))],
        compiler_params=pltpu.CompilerParams(vmem_limit_bytes=1 << 20),
        cost_estimate=pl.CostEstimate(flops=0, bytes_accessed=8 * blocks.size, transcendentals=0),
    )(columns, blocks)


def placed_by_core(blocks, columns, core, extra=None):
    count, rows, width = blocks.shape
    arrays = [blocks] if extra is None else [blocks, extra]
    more = 0 if extra is None else extra.shape[0] // count

    def kernel(where_ref, blocks_ref, *rest):
        kept_ref, sent_ref, done = rest[-3:]
        core = where_ref[count]

        def place(source, device, span, semaphore):
            kept, sent = (
                pltpu.make_async_copy(source, ref.at[device // 2, span], semaphore)
                for ref in (kept_ref, sent_ref)
            )
            pl.when(device % 2 == core)(kept.start)
            pl.when(device % 2 != core)(sent.start)
            return kept

        copies = []
        for i in range(count):
            copies.append(place(blocks_ref.at[i], where_ref[i], pl.ds(0, rows), done.at[i]))
            if more:
                part = rest[0].at[pl.ds(i * more, more)]
                copies.append(place(part, jnp.int32(i), pl.ds(rows, more), done.at[count + i]))
        for copy in copies:
            copy.wait()

    out = jax.ShapeDtypeStruct((count // 2, rows + more, width), blocks.dtype)
    return pl.pallas_call(
        kernel,
        out_shape=[out, out],
        in_specs=[pl.BlockSpec(memory_space=pltpu.SMEM)]
        + [pl.BlockSpec(memory_space=pl.ANY)] * len(arrays),
        out_specs=[pl.BlockSpec(memory_space=pl.ANY)] * 2,
        scratch_shapes=[pltpu.SemaphoreType.DMA((len(arrays) * count,))],
        compiler_params=pltpu.CompilerParams(vmem_limit_bytes=1 << 20),
        cost_estimate=pl.CostEstimate(flops=0, bytes_accessed=8 * blocks.size, transcendentals=0),
    )(jnp.concatenate([columns, core[None]]), *arrays)


def high_low(value):
    high = value.astype(jnp.bfloat16)
    return high, (value - high.astype(jnp.float32)).astype(jnp.bfloat16)


def product_of(left, right):
    return jnp.dot(left, right, preferred_element_type=jnp.float32)


def kernel_cost(tile, width):
    return pl.CostEstimate(flops=3 * tile.size * width, bytes_accessed=2 * tile.size, transcendentals=0)


def direct_quarters(tile, column_block, quarters, places):
    each, _, _, rows, order = tile.shape
    width = column_block.shape[1]
    steps = len(quarters)

    def kernel(where_ref, tile_ref, column_ref, *rest):
        out_refs, both = rest[:-1], rest[-1]
        step = pl.program_id(0)

        @pl.when(step == 0)
        def _():
            high, low = high_low(column_ref[...])
            both[:, :width] = high
            both[:, width:] = low

        high, low = high_low(tile_ref[...].reshape(each * rows, order))
        wide = product_of(high, both[...])
        total = wide[:, :width] + wide[:, width:] + product_of(low, both[:, :width])
        for g, out_ref in enumerate(out_refs):

            @pl.when(step == g)
            def _():
                for k in range(each):
                    out_ref[where_ref[2 * steps + k]] = total[k * rows : (k + 1) * rows]

    return pl.pallas_call(
        kernel,
        out_shape=[jax.ShapeDtypeStruct((each, rows, width), jnp.float32)] * steps,
        grid_spec=pltpu.PrefetchScalarGridSpec(
            num_scalar_prefetch=1,
            grid=(steps,),
            in_specs=[
                pl.BlockSpec(
                    (each, 1, 1, rows, order), lambda g, where: (0, where[2 * g], where[2 * g + 1], 0, 0)
                ),
                pl.BlockSpec((order, width), lambda g, where: (0, 0)),
            ],
            out_specs=[pl.BlockSpec((each, rows, width), lambda g, where: (0, 0, 0))] * steps,
            scratch_shapes=[pltpu.VMEM((order, 2 * width), jnp.bfloat16)],
        ),
        compiler_params=pltpu.CompilerParams(vmem_limit_bytes=60 << 20),
        cost_estimate=pl.CostEstimate(
            flops=3 * steps * each * rows * order * width,
            bytes_accessed=4 * steps * each * rows * order,
            transcendentals=0,
        ),
    )(jnp.concatenate([jnp.stack([bit for pair in quarters for bit in pair]), places]), tile, column_block)


def transposed_half(tile, quarters, half, spots, partial=None):
    groups, _, rows, order = tile.shape
    width = quarters[0].shape[2]
    depth = groups * rows
    each = groups // 2
    steps = 3
    chunk = order // steps

    def kernel(where_ref, tile_ref, first_ref, second_ref, *rest):
        partial_ref, (out_ref, gathered, both) = (rest[0], rest[1:]) if partial is not None else (None, rest)

        @pl.when(pl.program_id(0) == 0)
        def _():
            for k in range(groups):
                spot = pl.multiple_of(where_ref[1 + k] * rows, rows)
                part = first_ref[k] if k < each else second_ref[k - each]
                gathered[pl.ds(spot, rows)] = part
            high, low = high_low(gathered[...].T)
            both[:width] = high
            both[width:] = low

        high, low = high_low(tile_ref[...].reshape(depth, chunk))
        wide = product_of(both[...], high)
        total = wide[:width] + wide[width:] + product_of(both[:width], low)
        if partial_ref is None:
            out_ref[...] = total
        else:
            out_ref[...] = (total + partial_ref[...]).T

    flat = pl.BlockSpec((width, chunk), lambda g, where: (0, g))
    return pl.pallas_call(
        kernel,
        out_shape=jax.ShapeDtypeStruct((width, order) if partial is None else (order, width), jnp.float32),
        grid_spec=pltpu.PrefetchScalarGridSpec(
            num_scalar_prefetch=1,
            grid=(steps,),
            in_specs=[
                pl.BlockSpec((groups, 1, rows, chunk), lambda g, where: (0, where[0], 0, g)),
            ]
            + [pl.BlockSpec((each, rows, width), lambda g, where: (0, 0, 0))] * 2
            + ([] if partial is None else [flat]),
            out_specs=flat if partial is None else pl.BlockSpec((chunk, width), lambda g, where: (g, 0)),
            scratch_shapes=[
                pltpu.VMEM((depth, width), jnp.float32),
                pltpu.VMEM((2 * width, depth), jnp.bfloat16),
            ],
        ),
        compiler_params=pltpu.CompilerParams(vmem_limit_bytes=60 << 20),
        cost_estimate=kernel_cost(tile, width),
    )(jnp.concatenate([half[None], spots]), tile, *quarters, *([] if partial is None else [partial]))


def swap(value, mask):
    size = lax.axis_size(NARROW)
    return lax.ppermute(value, NARROW, [(i, i ^ mask) for i in range(size)])


ENTRIES = (8, 4, 12)
REVERSED = (0, 4, 2, 6, 1, 5, 3, 7)
REVERSED_PAIR = (0, 2, 1, 3)


def summed_part(kept):
    total = kept[0]
    for k, mask in enumerate(ENTRIES):
        total = total + swap(kept[k + 1], mask)
    return total


def apply_hamiltonian(tile, columns, vectors, want_gram):
    rows, width = vectors.shape
    count = lax.axis_size(NARROW)
    order = count * rows
    groups = count // 2
    me = lax.axis_index(NARROW).astype(jnp.int32)
    near, far = me & 1, (me & 1) ^ 1
    table = jnp.array(REVERSED, jnp.int32)
    spots = table ^ (me >> 1)
    tile = tile.reshape(groups, 2, rows, order)
    with jax.named_scope("gather_wide"):
        slices = to_everyone(vectors, WIDE)
    with jax.named_scope("gather_row"):
        quarter = jnp.stack([vectors] + [swap(vectors, mask) for mask in ENTRIES])
        near_rows, far_rows = [quarter, swap(quarter, 2)], [swap(quarter, 1)]
        slices, near_rows, far_rows = lax.optimization_barrier((slices, near_rows, far_rows))
        far_rows.append(swap(near_rows[1], 1))
    with jax.named_scope("gather_column"):
        picked = picked_blocks(slices, columns)
        column_block = exchange(picked, NARROW).reshape(order, width)
    with jax.named_scope("transposed"):
        partial = transposed_half(tile, near_rows, near, spots)
        transposed = transposed_half(tile, far_rows, far, spots, partial)
        transposed, column_block = lax.optimization_barrier((transposed, column_block))
    with jax.named_scope("back_transposed"):
        arrived = exchange(transposed.reshape(count, rows, width), NARROW)
    with jax.named_scope("direct"):
        quarters = tile.reshape(groups // 2, 2, 2, rows, order)
        first, second = (me >> 1) & 1, ((me >> 1) & 1) ^ 1
        high_bits = me >> 2
        places = jnp.array(REVERSED_PAIR, jnp.int32) ^ ((high_bits & 1) << 1 | high_bits >> 1)
        (far_second,) = direct_quarters(quarters, column_block, [(second, far)], places)
        column_block, far_second = lax.optimization_barrier((column_block, far_second))
        got_second = swap(far_second, 1)
        far_first, near_second = direct_quarters(
            quarters, column_block, [(first, far), (second, near)], places
        )
        column_block, far_first = lax.optimization_barrier((column_block, far_first))
        got_first = swap(far_first, 1)
        (near_first,) = direct_quarters(quarters, column_block, [(first, near)], places)
        kept = near_first + got_first + swap(near_second + got_second, 2)
        arrived, kept = lax.optimization_barrier((arrived, kept))
    gram = None
    if want_gram:
        with jax.named_scope("gram_block_row"):
            block, _ = lax.optimization_barrier((near_rows + far_rows, near_first))
            gram = sum(gram_of(quarter.reshape(-1, width)) for quarter in block)
    with jax.named_scope("back_direct"):
        direct_sum = summed_part(kept)
    with jax.named_scope("back_wide"):
        core = lax.axis_index(CORE).astype(jnp.int32)
        kept, sent = placed_by_core(arrived, columns, core, extra=gram)
        kept = kept + lax.ppermute(sent, CORE, [(0, 1), (1, 0)])
        sums = exchange(kept, CHIP).sum(axis=0)
    return direct_sum + sums[:rows], sums[rows:]


def exact(left, right):
    return jnp.dot(left, right, precision=HIGHEST, preferred_element_type=jnp.float32)


def inverse_root(gram, total_rows):
    width = gram.shape[0]
    row = lax.broadcasted_iota(jnp.int32, (width, width), 0)
    identity = (row == lax.broadcasted_iota(jnp.int32, (width, width), 1)).astype(jnp.float32)
    scale = jnp.sqrt(jnp.sum(gram * gram, keepdims=True) + 1e-06)
    current = gram / scale
    inverse = identity
    for repeat in range(NS_STEPS):
        middle = 1.5 * identity - 0.5 * exact(inverse, current)
        current = exact(current, middle)
        inverse = exact(middle, inverse)
    return inverse * jnp.sqrt(total_rows / scale)


def in_kernel(function, shape, *arrays):
    def kernel(*refs):
        refs[-1][...] = function(*(ref[...] for ref in refs[:-1]))

    return pl.pallas_call(
        kernel,
        out_shape=jax.ShapeDtypeStruct(shape, jnp.float32),
        cost_estimate=pl.CostEstimate(flops=1 << 30, bytes_accessed=1 << 20, transcendentals=0),
    )(*arrays)


def gram_of(value):
    return lax.dot_general(value, value, (((0,), (0,)), ((), ())), precision=HIGHEST)


def on_device(tile, row_columns, start_vectors):
    total_rows = float(lax.axis_size(WIDE) * lax.axis_size(NARROW) * start_vectors.shape[0])
    columns = row_columns[0]
    first, _ = apply_hamiltonian(tile, columns, start_vectors, want_gram=False)
    second, gram_rows = apply_hamiltonian(tile, columns, first, want_gram=True)
    width = second.shape[1]
    wide = lax.axis_size(WIDE)
    with jax.named_scope("gram_sum_wide"):
        parts = gram_of(second).reshape(wide, width // wide, width)
        given = jnp.broadcast_to(gram_rows[None], parts.shape)
        got = exchange(jnp.concatenate([parts, given], axis=1), WIDE)
        gram_second = got[:, : width // wide].sum(axis=0)
        gram_first = got[:, width // wide :].reshape(width, width)
    with jax.named_scope("gram_sum_narrow"):
        gram_second = to_everyone(gram_second, NARROW).sum(axis=0)
    with jax.named_scope("inverse_first"):
        root_first = in_kernel(lambda gram: inverse_root(gram, total_rows), (width, width), gram_first)
    with jax.named_scope("gram_whole"):
        gram_second = to_everyone(gram_second, WIDE).reshape(width, width)

    def finish(gram, root, value):
        gram = exact(root.T, exact(gram, root))
        return exact(exact(value, root), inverse_root(gram, total_rows))

    with jax.named_scope("finish"):
        return in_kernel(finish, second.shape, gram_second, root_first, second)


def solution(mesh):
    wide, narrow = mesh.devices.shape
    finer = Mesh(mesh.devices.reshape(wide // 2, 2, narrow), (CHIP, CORE, NARROW))
    return jax.shard_map(
        on_device,
        mesh=finer,
        in_specs=(P(WIDE, NARROW), P(WIDE, None), P((CHIP, CORE, NARROW), None)),
        out_specs=P((CHIP, CORE, NARROW), None),
        check_vma=False,
    )
```

```python
import jax
import jax.numpy as jnp
from jax import lax
from jax.experimental import pallas as pl
from jax.experimental.pallas import tpu as pltpu
from jax.sharding import PartitionSpec as P

NS_STEPS = 5
WIDE, NARROW = "wide", "narrow"
HIGHEST = lax.Precision.HIGHEST


def exchange(parts, axis):
    return lax.all_to_all(parts, axis, 0, 0, tiled=True)


def to_everyone(value, axis):
    return exchange(jnp.broadcast_to(value[None], (lax.axis_size(axis), *value.shape)), axis)


def move_blocks(blocks, columns, scatter, extra=None):
    count, rows, width = blocks.shape
    arrays = [blocks] if extra is None else [blocks, extra]
    more = 0 if extra is None else extra.shape[0] // count

    def kernel(columns_ref, blocks_ref, *rest):
        moved_ref, done = rest[-2:]
        copies = []
        for i in range(count):
            column = columns_ref[i]
            source, target = (i, column) if scatter else (column, i)
            copies.append(
                pltpu.make_async_copy(
                    blocks_ref.at[source], moved_ref.at[target, pl.ds(0, rows)], done.at[i]
                )
            )
            if more:
                copies.append(
                    pltpu.make_async_copy(
                        rest[0].at[pl.ds(i * more, more)],
                        moved_ref.at[i, pl.ds(rows, more)],
                        done.at[count + i],
                    )
                )
        for copy in copies:
            copy.start()
        for copy in copies:
            copy.wait()

    return pl.pallas_call(
        kernel,
        out_shape=jax.ShapeDtypeStruct((count, rows + more, width), blocks.dtype),
        in_specs=[pl.BlockSpec(memory_space=pltpu.SMEM)]
        + [pl.BlockSpec(memory_space=pl.ANY)] * len(arrays),
        out_specs=pl.BlockSpec(memory_space=pl.ANY),
        scratch_shapes=[pltpu.SemaphoreType.DMA((len(arrays) * count,))],
        compiler_params=pltpu.CompilerParams(vmem_limit_bytes=1 << 20),
        cost_estimate=pl.CostEstimate(flops=0, bytes_accessed=8 * blocks.size, transcendentals=0),
    )(columns, *arrays)


def high_low(value):
    high = value.astype(jnp.bfloat16)
    return high, (value - high.astype(jnp.float32)).astype(jnp.bfloat16)


def product_of(left, right):
    return jnp.dot(left, right, preferred_element_type=jnp.float32)


def kernel_cost(tile, width):
    return pl.CostEstimate(flops=3 * tile.size * width, bytes_accessed=2 * tile.size, transcendentals=0)


def direct_quarters(tile, column_block, quarters, where):
    each, _, _, rows, order = tile.shape
    width = column_block.shape[1]
    steps = len(quarters)

    def second_of(g):
        return quarters[0][0] + g * (quarters[-1][0] - quarters[0][0])

    def far_of(g):
        return quarters[0][1] + g * (quarters[-1][1] - quarters[0][1])

    def kernel(where_ref, tile_ref, column_ref, *rest):
        out_refs, both = rest[:-1], rest[-1]
        step = pl.program_id(0)

        @pl.when(step == 0)
        def _():
            high, low = high_low(column_ref[...])
            both[:, :width] = high
            both[:, width:] = low

        high, low = high_low(tile_ref[...].reshape(each * rows, order))
        wide = product_of(high, both[...])
        total = wide[:, :width] + wide[:, width:] + product_of(low, both[:, :width])
        for g, out_ref in enumerate(out_refs):

            @pl.when(step == g)
            def _():
                for k in range(each):
                    out_ref[where_ref[PLACES + k]] = total[k * rows : (k + 1) * rows]

    return pl.pallas_call(
        kernel,
        out_shape=[jax.ShapeDtypeStruct((each, rows, width), jnp.float32)] * steps,
        grid_spec=pltpu.PrefetchScalarGridSpec(
            num_scalar_prefetch=1,
            grid=(steps,),
            in_specs=[
                pl.BlockSpec(
                    (each, 1, 1, rows, order),
                    lambda g, where: (0, where[HALVES + 2] ^ second_of(g), where[HALVES] ^ far_of(g), 0, 0),
                ),
                pl.BlockSpec((order, width), lambda g, where: (0, 0)),
            ],
            out_specs=[pl.BlockSpec((each, rows, width), lambda g, where: (0, 0, 0))] * steps,
            scratch_shapes=[pltpu.VMEM((order, 2 * width), jnp.bfloat16)],
        ),
        compiler_params=pltpu.CompilerParams(vmem_limit_bytes=50 << 20),
        cost_estimate=pl.CostEstimate(
            flops=3 * steps * each * rows * order * width,
            bytes_accessed=4 * steps * each * rows * order,
            transcendentals=0,
        ),
    )(where, tile, column_block)


def transposed_half(tile, quarters, half, where, partial=None):
    groups, _, rows, order = tile.shape
    width = quarters[0].shape[2]
    depth = groups * rows
    each = groups // 2
    steps = 3
    chunk = order // steps

    def kernel(where_ref, tile_ref, first_ref, second_ref, *rest):
        partial_ref, (out_ref, gathered, both) = (rest[0], rest[1:]) if partial is not None else (None, rest)

        @pl.when(pl.program_id(0) == 0)
        def _():
            for k in range(groups):
                spot = pl.multiple_of(where_ref[SPOTS + k] * rows, rows)
                part = first_ref[k] if k < each else second_ref[k - each]
                gathered[pl.ds(spot, rows)] = part
            high, low = high_low(gathered[...].T)
            both[:width] = high
            both[width:] = low

        high, low = high_low(tile_ref[...].reshape(depth, chunk))
        wide = product_of(both[...], high)
        total = wide[:width] + wide[width:] + product_of(both[:width], low)
        if partial_ref is None:
            out_ref[...] = total
        else:
            out_ref[...] = (total + partial_ref[...]).T

    flat = pl.BlockSpec((width, chunk), lambda g, where: (0, g))
    return pl.pallas_call(
        kernel,
        out_shape=jax.ShapeDtypeStruct((width, order) if partial is None else (order, width), jnp.float32),
        grid_spec=pltpu.PrefetchScalarGridSpec(
            num_scalar_prefetch=1,
            grid=(steps,),
            in_specs=[
                pl.BlockSpec((groups, 1, rows, chunk), lambda g, where: (0, where[HALVES + half], 0, g)),
            ]
            + [pl.BlockSpec((each, rows, width), lambda g, where: (0, 0, 0))] * 2
            + ([] if partial is None else [flat]),
            out_specs=flat if partial is None else pl.BlockSpec((chunk, width), lambda g, where: (g, 0)),
            scratch_shapes=[
                pltpu.VMEM((depth, width), jnp.float32),
                pltpu.VMEM((2 * width, depth), jnp.bfloat16),
            ],
        ),
        compiler_params=pltpu.CompilerParams(vmem_limit_bytes=50 << 20),
        cost_estimate=kernel_cost(tile, width),
    )(where, tile, *quarters, *([] if partial is None else [partial]))


def swap(value, mask):
    size = lax.axis_size(NARROW)
    return lax.ppermute(value, NARROW, [(i, i ^ mask) for i in range(size)])


ENTRIES = (8, 4, 12)
REVERSED = (0, 4, 2, 6, 1, 5, 3, 7)
REVERSED_PAIR = (0, 2, 1, 3)

HALVES, SPOTS, PLACES = 0, 3, 11


def kernel_indices(me):
    high_bits = me >> 2
    return jnp.concatenate(
        [
            jnp.stack([me & 1, (me & 1) ^ 1, (me >> 1) & 1]),
            jnp.array(REVERSED, jnp.int32) ^ (me >> 1),
            jnp.array(REVERSED_PAIR, jnp.int32) ^ ((high_bits & 1) << 1 | high_bits >> 1),
        ]
    )


def summed_part(kept):
    total = kept[0]
    for k, mask in enumerate(ENTRIES):
        total = total + swap(kept[k + 1], mask)
    return total


def apply_hamiltonian(tile, columns, where, vectors, want_gram):
    rows, width = vectors.shape
    count = lax.axis_size(NARROW)
    order = count * rows
    groups = count // 2
    tile = tile.reshape(groups, 2, rows, order)
    with jax.named_scope("gather_wide"):
        slices = to_everyone(vectors, WIDE)
    with jax.named_scope("gather_row"):
        quarter = jnp.stack([vectors] + [swap(vectors, mask) for mask in ENTRIES])
        near_rows, far_rows = [quarter, swap(quarter, 2)], [swap(quarter, 1)]
        slices, near_rows, far_rows = lax.optimization_barrier((slices, near_rows, far_rows))
        far_rows.append(swap(near_rows[1], 1))
    with jax.named_scope("gather_column"):
        picked = move_blocks(slices, columns, scatter=False)
        column_block = exchange(picked, NARROW).reshape(order, width)
    with jax.named_scope("transposed"):
        partial = transposed_half(tile, near_rows, 0, where)
        transposed = transposed_half(tile, far_rows, 1, where, partial)
        transposed, column_block = lax.optimization_barrier((transposed, column_block))
    with jax.named_scope("back_transposed"):
        arrived = exchange(transposed.reshape(count, rows, width), NARROW)
    with jax.named_scope("direct"):
        quarters = tile.reshape(groups // 2, 2, 2, rows, order)
        (far_second,) = direct_quarters(quarters, column_block, [(1, 1)], where)
        column_block, far_second = lax.optimization_barrier((column_block, far_second))
        got_second = swap(far_second, 1)
        far_first, near_second = direct_quarters(
            quarters, column_block, [(0, 1), (1, 0)], where
        )
        column_block, far_first = lax.optimization_barrier((column_block, far_first))
        got_first = swap(far_first, 1)
        (near_first,) = direct_quarters(quarters, column_block, [(0, 0)], where)
        kept = near_first + got_first + swap(near_second + got_second, 2)
        arrived, kept = lax.optimization_barrier((arrived, kept))
    gram = None
    if want_gram:
        with jax.named_scope("gram_block_row"):
            block, _ = lax.optimization_barrier((near_rows + far_rows, near_first))
            gram = sum(gram_of(quarter.reshape(-1, width)) for quarter in block)
    with jax.named_scope("back_direct"):
        direct_sum = summed_part(kept)
    with jax.named_scope("back_wide"):
        placed = move_blocks(arrived, columns, scatter=True, extra=gram)
        sums = exchange(placed, WIDE).sum(axis=0)
    return direct_sum + sums[:rows], sums[rows:]


def exact(left, right):
    return jnp.dot(left, right, precision=HIGHEST, preferred_element_type=jnp.float32)


def inverse_root(gram, total_rows):
    width = gram.shape[0]
    row = lax.broadcasted_iota(jnp.int32, (width, width), 0)
    identity = (row == lax.broadcasted_iota(jnp.int32, (width, width), 1)).astype(jnp.float32)
    scale = jnp.sqrt(jnp.sum(gram * gram, keepdims=True) + 1e-06)
    current = gram / scale
    inverse = None
    for repeat in range(NS_STEPS):
        middle = 1.5 * identity - 0.5 * (current if repeat == 0 else exact(inverse, current))
        if repeat + 1 < NS_STEPS:
            current = exact(current, middle)
        inverse = middle if repeat == 0 else exact(middle, inverse)
    return inverse * jnp.sqrt(total_rows / scale)


def in_kernel(function, shapes, *arrays):
    def kernel(*refs):
        results = function(*(ref[...] for ref in refs[: len(arrays)]))
        for ref, result in zip(refs[len(arrays) :], results):
            ref[...] = result

    return pl.pallas_call(
        kernel,
        out_shape=[jax.ShapeDtypeStruct(shape, jnp.float32) for shape in shapes],
        compiler_params=pltpu.CompilerParams(vmem_limit_bytes=8 << 20),
        cost_estimate=pl.CostEstimate(flops=1 << 30, bytes_accessed=1 << 20, transcendentals=0),
    )(*arrays)


def gram_of(value):
    return lax.dot_general(value, value, (((0,), (0,)), ((), ())), precision=HIGHEST)


def on_device(tile, row_columns, start_vectors):
    total_rows = float(lax.axis_size(WIDE) * lax.axis_size(NARROW) * start_vectors.shape[0])
    columns = row_columns[0]
    where = kernel_indices(lax.axis_index(NARROW).astype(jnp.int32))
    first, _ = apply_hamiltonian(tile, columns, where, start_vectors, want_gram=False)
    second, gram_rows = apply_hamiltonian(tile, columns, where, first, want_gram=True)
    width = second.shape[1]
    wide = lax.axis_size(WIDE)
    with jax.named_scope("gram_sum_wide"):
        parts = gram_of(second).reshape(wide, width // wide, width)
        given = jnp.broadcast_to(gram_rows[None], parts.shape)
        got = exchange(jnp.concatenate([parts, given], axis=1), WIDE)
        gram_second = got[:, : width // wide].sum(axis=0)
        gram_first = got[:, width // wide :].reshape(width, width)
    with jax.named_scope("gram_sum_narrow"):
        gram_second = to_everyone(gram_second, NARROW).sum(axis=0)
    def begin(gram, value):
        root = inverse_root(gram, total_rows)
        return root, exact(value, root)

    def finish(gram, root, value):
        gram = exact(root.T, exact(gram, root))
        return (exact(value, inverse_root(gram, total_rows)),)

    with jax.named_scope("inverse_first"):
        root_first, second = in_kernel(begin, [(width, width), second.shape], gram_first, second)
    with jax.named_scope("gram_whole"):
        gram_second = to_everyone(gram_second, WIDE).reshape(width, width)
    with jax.named_scope("finish"):
        return in_kernel(finish, [second.shape], gram_second, root_first, second)[0]


def solution(mesh):
    return jax.shard_map(
        on_device,
        mesh=mesh,
        in_specs=(P(WIDE, NARROW), P(WIDE, None), P((WIDE, NARROW), None)),
        out_specs=P((WIDE, NARROW), None),
        check_vma=False,
    )
```

```python
import jax
import jax.numpy as jnp
from jax import lax
from jax.experimental import pallas as pl
from jax.experimental.pallas import tpu as pltpu
from jax.sharding import PartitionSpec as P

NS_STEPS = 5
WIDE, NARROW = "wide", "narrow"
HIGHEST = lax.Precision.HIGHEST


def exchange(parts, axis):
    return lax.all_to_all(parts, axis, 0, 0, tiled=True)


def to_everyone(value, axis):
    return exchange(jnp.broadcast_to(value[None], (lax.axis_size(axis), *value.shape)), axis)


def move_blocks(blocks, columns, scatter, extra=None):
    count, rows, width = blocks.shape
    arrays = [blocks] if extra is None else [blocks, extra]
    more = 0 if extra is None else extra.shape[0] // count

    def kernel(columns_ref, blocks_ref, *rest):
        moved_ref, done = rest[-2:]
        copies = []
        for i in range(count):
            column = columns_ref[0, i]
            source, target = (i, column) if scatter else (column, i)
            copies.append(
                pltpu.make_async_copy(
                    blocks_ref.at[source], moved_ref.at[target, pl.ds(0, rows)], done.at[i]
                )
            )
            if more:
                copies.append(
                    pltpu.make_async_copy(
                        rest[0].at[pl.ds(i * more, more)],
                        moved_ref.at[i, pl.ds(rows, more)],
                        done.at[count + i],
                    )
                )
        for copy in copies:
            copy.start()
        for copy in copies:
            copy.wait()

    return pl.pallas_call(
        kernel,
        out_shape=jax.ShapeDtypeStruct((count, rows + more, width), blocks.dtype),
        in_specs=[pl.BlockSpec(memory_space=pltpu.SMEM)]
        + [pl.BlockSpec(memory_space=pl.ANY)] * len(arrays),
        out_specs=pl.BlockSpec(memory_space=pl.ANY),
        scratch_shapes=[pltpu.SemaphoreType.DMA((len(arrays) * count,))],
        compiler_params=pltpu.CompilerParams(vmem_limit_bytes=1 << 20),
        cost_estimate=pl.CostEstimate(flops=0, bytes_accessed=8 * blocks.size, transcendentals=0),
    )(columns, *arrays)


def high_low(value):
    high = value.astype(jnp.bfloat16)
    return high, (value - high.astype(jnp.float32)).astype(jnp.bfloat16)


def product_of(left, right):
    return jnp.dot(left, right, preferred_element_type=jnp.float32)


def kernel_cost(tile, width):
    return pl.CostEstimate(flops=3 * tile.size * width, bytes_accessed=2 * tile.size, transcendentals=0)


def direct_quarters(tile, column_block, quarters, where):
    each, _, _, rows, order = tile.shape
    width = column_block.shape[1]
    steps = len(quarters)

    def second_of(g):
        return quarters[0][0] + g * (quarters[-1][0] - quarters[0][0])

    def far_of(g):
        return quarters[0][1] + g * (quarters[-1][1] - quarters[0][1])

    def kernel(where_ref, tile_ref, column_ref, *rest):
        out_refs, both = rest[:-1], rest[-1]
        step = pl.program_id(0)

        @pl.when(step == 0)
        def _():
            high, low = high_low(column_ref[...])
            both[:, :width] = high
            both[:, width:] = low

        high, low = high_low(tile_ref[...].reshape(each * rows, order))
        wide = product_of(high, both[...])
        total = wide[:, :width] + wide[:, width:] + product_of(low, both[:, :width])
        for g, out_ref in enumerate(out_refs):

            @pl.when(step == g)
            def _():
                for k in range(each):
                    out_ref[where_ref[PLACES + k]] = total[k * rows : (k + 1) * rows]

    return pl.pallas_call(
        kernel,
        out_shape=[jax.ShapeDtypeStruct((each, rows, width), jnp.float32)] * steps,
        grid_spec=pltpu.PrefetchScalarGridSpec(
            num_scalar_prefetch=1,
            grid=(steps,),
            in_specs=[
                pl.BlockSpec(
                    (each, 1, 1, rows, order),
                    lambda g, where: (0, where[HALVES + 2] ^ second_of(g), where[HALVES] ^ far_of(g), 0, 0),
                ),
                pl.BlockSpec((order, width), lambda g, where: (0, 0)),
            ],
            out_specs=[pl.BlockSpec((each, rows, width), lambda g, where: (0, 0, 0))] * steps,
            scratch_shapes=[pltpu.VMEM((order, 2 * width), jnp.bfloat16)],
        ),
        compiler_params=pltpu.CompilerParams(vmem_limit_bytes=50 << 20),
        cost_estimate=pl.CostEstimate(
            flops=3 * steps * each * rows * order * width,
            bytes_accessed=4 * steps * each * rows * order,
            transcendentals=0,
        ),
    )(where, tile, column_block)


def transposed_half(tile, quarters, half, where, partial=None):
    groups, _, rows, order = tile.shape
    width = quarters[0].shape[2]
    depth = groups * rows
    each = groups // 2
    steps = 3
    chunk = order // steps

    def kernel(where_ref, tile_ref, first_ref, second_ref, *rest):
        partial_ref, (out_ref, gathered, both) = (rest[0], rest[1:]) if partial is not None else (None, rest)

        @pl.when(pl.program_id(0) == 0)
        def _():
            for k in range(groups):
                spot = pl.multiple_of(where_ref[SPOTS + k] * rows, rows)
                part = first_ref[k] if k < each else second_ref[k - each]
                gathered[pl.ds(spot, rows)] = part
            high, low = high_low(gathered[...].T)
            both[:width] = high
            both[width:] = low

        high, low = high_low(tile_ref[...].reshape(depth, chunk))
        wide = product_of(both[...], high)
        total = wide[:width] + wide[width:] + product_of(both[:width], low)
        if partial_ref is None:
            out_ref[...] = total
        else:
            out_ref[...] = (total + partial_ref[...]).T

    flat = pl.BlockSpec((width, chunk), lambda g, where: (0, g))
    return pl.pallas_call(
        kernel,
        out_shape=jax.ShapeDtypeStruct((width, order) if partial is None else (order, width), jnp.float32),
        grid_spec=pltpu.PrefetchScalarGridSpec(
            num_scalar_prefetch=1,
            grid=(steps,),
            in_specs=[
                pl.BlockSpec((groups, 1, rows, chunk), lambda g, where: (0, where[HALVES + half], 0, g)),
            ]
            + [pl.BlockSpec((each, rows, width), lambda g, where: (0, 0, 0))] * 2
            + ([] if partial is None else [flat]),
            out_specs=flat if partial is None else pl.BlockSpec((chunk, width), lambda g, where: (g, 0)),
            scratch_shapes=[
                pltpu.VMEM((depth, width), jnp.float32),
                pltpu.VMEM((2 * width, depth), jnp.bfloat16),
            ],
        ),
        compiler_params=pltpu.CompilerParams(vmem_limit_bytes=50 << 20),
        cost_estimate=kernel_cost(tile, width),
    )(where, tile, *quarters, *([] if partial is None else [partial]))


def swap(value, mask):
    size = lax.axis_size(NARROW)
    return lax.ppermute(value, NARROW, [(i, i ^ mask) for i in range(size)])


ENTRIES = (8, 4, 12)
REVERSED = (0, 4, 2, 6, 1, 5, 3, 7)
REVERSED_PAIR = (0, 2, 1, 3)

HALVES, SPOTS, PLACES = 0, 3, 11


def kernel_indices(me):
    high_bits = me >> 2
    return jnp.concatenate(
        [
            jnp.stack([me & 1, (me & 1) ^ 1, (me >> 1) & 1]),
            jnp.array(REVERSED, jnp.int32) ^ (me >> 1),
            jnp.array(REVERSED_PAIR, jnp.int32) ^ ((high_bits & 1) << 1 | high_bits >> 1),
        ]
    )


def summed_part(kept):
    total = kept[0]
    for k, mask in enumerate(ENTRIES):
        total = total + swap(kept[k + 1], mask)
    return total


def apply_hamiltonian(tile, columns, where, vectors, want_gram):
    rows, width = vectors.shape
    count = lax.axis_size(NARROW)
    order = count * rows
    groups = count // 2
    tile = tile.reshape(groups, 2, rows, order)
    with jax.named_scope("gather_wide"):
        slices = to_everyone(vectors, WIDE)
    with jax.named_scope("gather_row"):
        quarter = jnp.stack([vectors] + [swap(vectors, mask) for mask in ENTRIES])
        near_rows, far_rows = [quarter, swap(quarter, 2)], [swap(quarter, 1)]
        slices, near_rows, far_rows = lax.optimization_barrier((slices, near_rows, far_rows))
        far_rows.append(swap(near_rows[1], 1))
    with jax.named_scope("gather_column"):
        picked = move_blocks(slices, columns, scatter=False)
        column_block = exchange(picked, NARROW).reshape(order, width)
    with jax.named_scope("transposed"):
        partial = transposed_half(tile, near_rows, 0, where)
        transposed = transposed_half(tile, far_rows, 1, where, partial)
        transposed, column_block = lax.optimization_barrier((transposed, column_block))
    with jax.named_scope("back_transposed"):
        arrived = exchange(transposed.reshape(count, rows, width), NARROW)
    with jax.named_scope("direct"):
        quarters = tile.reshape(groups // 2, 2, 2, rows, order)
        (far_second,) = direct_quarters(quarters, column_block, [(1, 1)], where)
        column_block, far_second = lax.optimization_barrier((column_block, far_second))
        got_second = swap(far_second, 1)
        far_first, near_second = direct_quarters(
            quarters, column_block, [(0, 1), (1, 0)], where
        )
        column_block, far_first = lax.optimization_barrier((column_block, far_first))
        got_first = swap(far_first, 1)
        (near_first,) = direct_quarters(quarters, column_block, [(0, 0)], where)
        kept = near_first + got_first + swap(near_second + got_second, 2)
        arrived, kept = lax.optimization_barrier((arrived, kept))
    gram = None
    if want_gram:
        with jax.named_scope("gram_block_row"):
            block, _ = lax.optimization_barrier((near_rows + far_rows, got_second))
            gram = sum(gram_of(quarter.reshape(-1, width)) for quarter in block)
    with jax.named_scope("back_direct"):
        direct_sum = summed_part(kept)
    with jax.named_scope("back_wide"):
        placed = move_blocks(arrived, columns, scatter=True, extra=gram)
        sums = exchange(placed, WIDE).sum(axis=0)
    return direct_sum + sums[:rows], sums[rows:]


def exact(left, right):
    return jnp.dot(left, right, precision=HIGHEST, preferred_element_type=jnp.float32)


def inverse_root(gram, total_rows):
    width = gram.shape[0]
    row = lax.broadcasted_iota(jnp.int32, (width, width), 0)
    identity = (row == lax.broadcasted_iota(jnp.int32, (width, width), 1)).astype(jnp.float32)
    scale = jnp.sqrt(jnp.sum(gram * gram, keepdims=True) + 1e-06)
    current = gram / scale
    inverse = None
    for repeat in range(NS_STEPS):
        middle = 1.5 * identity - 0.5 * (current if repeat == 0 else exact(inverse, current))
        if repeat + 1 < NS_STEPS:
            current = exact(current, middle)
        inverse = middle if repeat == 0 else exact(middle, inverse)
    return inverse * jnp.sqrt(total_rows / scale)


def in_kernel(function, shapes, *arrays):
    def kernel(*refs):
        results = function(*(ref[...] for ref in refs[: len(arrays)]))
        for ref, result in zip(refs[len(arrays) :], results):
            ref[...] = result

    return pl.pallas_call(
        kernel,
        out_shape=[jax.ShapeDtypeStruct(shape, jnp.float32) for shape in shapes],
        compiler_params=pltpu.CompilerParams(vmem_limit_bytes=8 << 20),
        cost_estimate=pl.CostEstimate(flops=1 << 30, bytes_accessed=1 << 20, transcendentals=0),
    )(*arrays)


def gram_of(value):
    return lax.dot_general(value, value, (((0,), (0,)), ((), ())), precision=HIGHEST)


def on_device(tile, row_columns, start_vectors):
    total_rows = float(lax.axis_size(WIDE) * lax.axis_size(NARROW) * start_vectors.shape[0])
    columns = row_columns
    where = kernel_indices(lax.axis_index(NARROW).astype(jnp.int32))
    first, _ = apply_hamiltonian(tile, columns, where, start_vectors, want_gram=False)
    second, gram_rows = apply_hamiltonian(tile, columns, where, first, want_gram=True)
    width = second.shape[1]
    wide = lax.axis_size(WIDE)
    with jax.named_scope("gram_sum_wide"):
        parts = gram_of(second).reshape(wide, width // wide, width)
        given = jnp.broadcast_to(gram_rows[None], parts.shape)
        got = exchange(jnp.concatenate([parts, given], axis=1), WIDE)
        gram_second = got[:, : width // wide].sum(axis=0)
        gram_first = got[:, width // wide :].reshape(width, width)
    with jax.named_scope("gram_sum_narrow"):
        gram_second = to_everyone(gram_second, NARROW).sum(axis=0)
    def begin(gram, value):
        root = inverse_root(gram, total_rows)
        return root, exact(value, root)

    def finish(gram, root, value):
        gram = exact(root.T, exact(gram, root))
        return (exact(value, inverse_root(gram, total_rows)),)

    with jax.named_scope("inverse_first"):
        root_first, second = in_kernel(begin, [(width, width), second.shape], gram_first, second)
    with jax.named_scope("gram_whole"):
        gram_second = to_everyone(gram_second, WIDE).reshape(width, width)
    with jax.named_scope("finish"):
        return in_kernel(finish, [second.shape], gram_second, root_first, second)[0]


def solution(mesh):
    return jax.shard_map(
        on_device,
        mesh=mesh,
        in_specs=(P(WIDE, NARROW), P(WIDE, None), P((WIDE, NARROW), None)),
        out_specs=P((WIDE, NARROW), None),
        check_vma=False,
    )
```

```python
import jax
import jax.numpy as jnp
from jax import lax
from jax.experimental import pallas as pl
from jax.experimental.pallas import tpu as pltpu
from jax.sharding import PartitionSpec as P

NS_STEPS = 5
WIDE, NARROW = "wide", "narrow"
HIGHEST = lax.Precision.HIGHEST


def exchange(parts, axis):
    return lax.all_to_all(parts, axis, 0, 0, tiled=True)


def to_everyone(value, axis):
    return exchange(jnp.broadcast_to(value[None], (lax.axis_size(axis), *value.shape)), axis)


def move_blocks(blocks, columns, scatter, extra=None):
    count, rows, width = blocks.shape
    arrays = [blocks] if extra is None else [blocks, extra]
    more = 0 if extra is None else extra.shape[0] // count

    def kernel(columns_ref, blocks_ref, *rest):
        moved_ref, done = rest[-2:]
        copies = []
        for i in range(count):
            column = columns_ref[0, i]
            source, target = (i, column) if scatter else (column, i)
            copies.append(
                pltpu.make_async_copy(
                    blocks_ref.at[source], moved_ref.at[target, pl.ds(0, rows)], done.at[i]
                )
            )
            if more:
                copies.append(
                    pltpu.make_async_copy(
                        rest[0].at[pl.ds(i * more, more)],
                        moved_ref.at[i, pl.ds(rows, more)],
                        done.at[count + i],
                    )
                )
        for copy in copies:
            copy.start()
        for copy in copies:
            copy.wait()

    return pl.pallas_call(
        kernel,
        out_shape=jax.ShapeDtypeStruct((count, rows + more, width), blocks.dtype),
        in_specs=[pl.BlockSpec(memory_space=pltpu.SMEM)]
        + [pl.BlockSpec(memory_space=pl.ANY)] * len(arrays),
        out_specs=pl.BlockSpec(memory_space=pl.ANY),
        scratch_shapes=[pltpu.SemaphoreType.DMA((len(arrays) * count,))],
        compiler_params=pltpu.CompilerParams(vmem_limit_bytes=1 << 20),
        cost_estimate=pl.CostEstimate(flops=0, bytes_accessed=8 * blocks.size, transcendentals=0),
    )(columns, *arrays)


def high_low(value):
    high = value.astype(jnp.bfloat16)
    return high, (value - high.astype(jnp.float32)).astype(jnp.bfloat16)


def product_of(left, right):
    return jnp.dot(left, right, preferred_element_type=jnp.float32)


def kernel_cost(tile, width):
    return pl.CostEstimate(flops=3 * tile.size * width, bytes_accessed=2 * tile.size, transcendentals=0)


def direct_quarters(tile, column_block, quarters, where):
    each, _, _, rows, order = tile.shape
    width = column_block.shape[1]
    steps = len(quarters)

    def second_of(g):
        return quarters[0][0] + g * (quarters[-1][0] - quarters[0][0])

    def far_of(g):
        return quarters[0][1] + g * (quarters[-1][1] - quarters[0][1])

    def kernel(where_ref, tile_ref, column_ref, *rest):
        out_refs, both = rest[:-1], rest[-1]
        step = pl.program_id(0)

        @pl.when(step == 0)
        def _():
            high, low = high_low(column_ref[...])
            both[:, :width] = high
            both[:, width:] = low

        high, low = high_low(tile_ref[...].reshape(each * rows, order))
        wide = product_of(high, both[...])
        total = wide[:, :width] + wide[:, width:] + product_of(low, both[:, :width])
        for g, out_ref in enumerate(out_refs):

            @pl.when(step == g)
            def _():
                for k in range(each):
                    out_ref[where_ref[PLACES + k]] = total[k * rows : (k + 1) * rows]

    return pl.pallas_call(
        kernel,
        out_shape=[jax.ShapeDtypeStruct((each, rows, width), jnp.float32)] * steps,
        grid_spec=pltpu.PrefetchScalarGridSpec(
            num_scalar_prefetch=1,
            grid=(steps,),
            in_specs=[
                pl.BlockSpec(
                    (each, 1, 1, rows, order),
                    lambda g, where: (0, where[HALVES + 2] ^ second_of(g), where[HALVES] ^ far_of(g), 0, 0),
                ),
                pl.BlockSpec((order, width), lambda g, where: (0, 0)),
            ],
            out_specs=[pl.BlockSpec((each, rows, width), lambda g, where: (0, 0, 0))] * steps,
            scratch_shapes=[pltpu.VMEM((order, 2 * width), jnp.bfloat16)],
        ),
        compiler_params=pltpu.CompilerParams(vmem_limit_bytes=50 << 20),
        cost_estimate=pl.CostEstimate(
            flops=3 * steps * each * rows * order * width,
            bytes_accessed=4 * steps * each * rows * order,
            transcendentals=0,
        ),
    )(where, tile, column_block)


def transposed_half(tile, quarters, half, where, partial=None):
    groups, _, rows, order = tile.shape
    width = quarters[0].shape[2]
    depth = groups * rows
    each = groups // 2
    steps = 3
    chunk = order // steps

    def kernel(where_ref, tile_ref, first_ref, second_ref, *rest):
        partial_ref, (out_ref, gathered, both) = (rest[0], rest[1:]) if partial is not None else (None, rest)

        @pl.when(pl.program_id(0) == 0)
        def _():
            for k in range(groups):
                spot = pl.multiple_of(where_ref[SPOTS + k] * rows, rows)
                part = first_ref[k] if k < each else second_ref[k - each]
                gathered[pl.ds(spot, rows)] = part
            high, low = high_low(gathered[...].T)
            both[:width] = high
            both[width:] = low

        high, low = high_low(tile_ref[...].reshape(depth, chunk))
        wide = product_of(both[...], high)
        total = wide[:width] + wide[width:] + product_of(both[:width], low)
        if partial_ref is None:
            out_ref[...] = total
        else:
            out_ref[...] = (total + partial_ref[...]).T

    flat = pl.BlockSpec((width, chunk), lambda g, where: (0, g))
    return pl.pallas_call(
        kernel,
        out_shape=jax.ShapeDtypeStruct((width, order) if partial is None else (order, width), jnp.float32),
        grid_spec=pltpu.PrefetchScalarGridSpec(
            num_scalar_prefetch=1,
            grid=(steps,),
            in_specs=[
                pl.BlockSpec((groups, 1, rows, chunk), lambda g, where: (0, where[HALVES + half], 0, g)),
            ]
            + [pl.BlockSpec((each, rows, width), lambda g, where: (0, 0, 0))] * 2
            + ([] if partial is None else [flat]),
            out_specs=flat if partial is None else pl.BlockSpec((chunk, width), lambda g, where: (g, 0)),
            scratch_shapes=[
                pltpu.VMEM((depth, width), jnp.float32),
                pltpu.VMEM((2 * width, depth), jnp.bfloat16),
            ],
        ),
        compiler_params=pltpu.CompilerParams(vmem_limit_bytes=50 << 20),
        cost_estimate=kernel_cost(tile, width),
    )(where, tile, *quarters, *([] if partial is None else [partial]))


def swap(value, mask):
    size = lax.axis_size(NARROW)
    return lax.ppermute(value, NARROW, [(i, i ^ mask) for i in range(size)])


ENTRIES = (8, 4, 12)
REVERSED = (0, 4, 2, 6, 1, 5, 3, 7)
REVERSED_PAIR = (0, 2, 1, 3)

HALVES, SPOTS, PLACES = 0, 3, 11


def kernel_indices(me):
    high_bits = me >> 2
    return jnp.concatenate(
        [
            jnp.stack([me & 1, (me & 1) ^ 1, (me >> 1) & 1]),
            jnp.array(REVERSED, jnp.int32) ^ (me >> 1),
            jnp.array(REVERSED_PAIR, jnp.int32) ^ ((high_bits & 1) << 1 | high_bits >> 1),
        ]
    )


def summed_part(kept):
    total = kept[0]
    for k, mask in enumerate(ENTRIES):
        total = total + swap(kept[k + 1], mask)
    return total


def apply_hamiltonian(tile, columns, where, vectors, want_gram):
    rows, width = vectors.shape
    count = lax.axis_size(NARROW)
    order = count * rows
    groups = count // 2
    tile = tile.reshape(groups, 2, rows, order)
    with jax.named_scope("gather_wide"):
        slices = to_everyone(vectors, WIDE)
    with jax.named_scope("gather_row"):
        quarter = jnp.stack([vectors] + [swap(vectors, mask) for mask in ENTRIES])
        near_rows, far_rows = [quarter, swap(quarter, 2)], [swap(quarter, 1)]
        slices, near_rows, far_rows = lax.optimization_barrier((slices, near_rows, far_rows))
        far_rows.append(swap(near_rows[1], 1))
    with jax.named_scope("gather_column"):
        picked = move_blocks(slices, columns, scatter=False)
        column_block = exchange(picked, NARROW).reshape(order, width)
    with jax.named_scope("transposed"):
        partial = transposed_half(tile, near_rows, 0, where)
        transposed = transposed_half(tile, far_rows, 1, where, partial)
        transposed, column_block = lax.optimization_barrier((transposed, column_block))
    with jax.named_scope("back_transposed"):
        arrived = exchange(transposed.reshape(count, rows, width), NARROW)
    with jax.named_scope("direct"):
        quarters = tile.reshape(groups // 2, 2, 2, rows, order)
        far_second, far_first = direct_quarters(quarters, column_block, [(1, 1), (0, 1)], where)
        column_block, far_second, far_first = lax.optimization_barrier(
            (column_block, far_second, far_first)
        )
        got_second, got_first = swap(far_second, 1), swap(far_first, 1)
        near_second, near_first = direct_quarters(
            quarters, column_block, [(1, 0), (0, 0)], where
        )
        kept = near_first + got_first + swap(near_second + got_second, 2)
        arrived, kept = lax.optimization_barrier((arrived, kept))
    gram = None
    if want_gram:
        with jax.named_scope("gram_block_row"):
            block, _ = lax.optimization_barrier((near_rows + far_rows, got_second))
            gram = sum(gram_of(quarter.reshape(-1, width)) for quarter in block)
    with jax.named_scope("back_direct"):
        direct_sum = summed_part(kept)
    with jax.named_scope("back_wide"):
        placed = move_blocks(arrived, columns, scatter=True, extra=gram)
        sums = exchange(placed, WIDE).sum(axis=0)
    return direct_sum + sums[:rows], sums[rows:]


def exact(left, right):
    return jnp.dot(left, right, precision=HIGHEST, preferred_element_type=jnp.float32)


def inverse_root(gram, total_rows):
    width = gram.shape[0]
    row = lax.broadcasted_iota(jnp.int32, (width, width), 0)
    identity = (row == lax.broadcasted_iota(jnp.int32, (width, width), 1)).astype(jnp.float32)
    scale = jnp.sqrt(jnp.sum(gram * gram, keepdims=True) + 1e-06)
    current = gram / scale
    inverse = None
    for repeat in range(NS_STEPS):
        middle = 1.5 * identity - 0.5 * (current if repeat == 0 else exact(inverse, current))
        if repeat + 1 < NS_STEPS:
            current = exact(current, middle)
        inverse = middle if repeat == 0 else exact(middle, inverse)
    return inverse * jnp.sqrt(total_rows / scale)


def in_kernel(function, shapes, *arrays):
    def kernel(*refs):
        results = function(*(ref[...] for ref in refs[: len(arrays)]))
        for ref, result in zip(refs[len(arrays) :], results):
            ref[...] = result

    return pl.pallas_call(
        kernel,
        out_shape=[jax.ShapeDtypeStruct(shape, jnp.float32) for shape in shapes],
        compiler_params=pltpu.CompilerParams(vmem_limit_bytes=8 << 20),
        cost_estimate=pl.CostEstimate(flops=1 << 30, bytes_accessed=1 << 20, transcendentals=0),
    )(*arrays)


def gram_of(value):
    return lax.dot_general(value, value, (((0,), (0,)), ((), ())), precision=HIGHEST)


def on_device(tile, row_columns, start_vectors):
    total_rows = float(lax.axis_size(WIDE) * lax.axis_size(NARROW) * start_vectors.shape[0])
    columns = row_columns
    where = kernel_indices(lax.axis_index(NARROW).astype(jnp.int32))
    first, _ = apply_hamiltonian(tile, columns, where, start_vectors, want_gram=False)
    second, gram_rows = apply_hamiltonian(tile, columns, where, first, want_gram=True)
    width = second.shape[1]
    wide = lax.axis_size(WIDE)
    with jax.named_scope("gram_sum_wide"):
        parts = gram_of(second).reshape(wide, width // wide, width)
        given = jnp.broadcast_to(gram_rows[None], parts.shape)
        got = exchange(jnp.concatenate([parts, given], axis=1), WIDE)
        gram_second = got[:, : width // wide].sum(axis=0)
        gram_first = got[:, width // wide :].reshape(width, width)
    with jax.named_scope("gram_sum_narrow"):
        gram_second = to_everyone(gram_second, NARROW).sum(axis=0)
    def begin(gram, value):
        root = inverse_root(gram, total_rows)
        return root, exact(value, root)

    def finish(gram, root, value):
        gram = exact(root.T, exact(gram, root))
        return (exact(value, inverse_root(gram, total_rows)),)

    with jax.named_scope("inverse_first"):
        root_first, second = in_kernel(begin, [(width, width), second.shape], gram_first, second)
    with jax.named_scope("gram_whole"):
        gram_second = to_everyone(gram_second, WIDE).reshape(width, width)
    with jax.named_scope("finish"):
        return in_kernel(finish, [second.shape], gram_second, root_first, second)[0]


def solution(mesh):
    return jax.shard_map(
        on_device,
        mesh=mesh,
        in_specs=(P(WIDE, NARROW), P(WIDE, None), P((WIDE, NARROW), None)),
        out_specs=P((WIDE, NARROW), None),
        check_vma=False,
    )
```
